256 devices in a mesh: pair: 2 (over z_hi), tensor: 4 (over x), dp: 32 (over y, z_lo, core).
Axes of the slice: x: 4, y: 4, z: 8 (z_hi: 2, z_lo: 4; z = z_hi * 4 + z_lo), core: 2. Of those that a mesh axis runs over, the one named last changes fastest.
Arguments:
- hidden_in: bfloat16 [32, 2, 384, 2560], P('dp', 'pair', 'tensor'), may hold values from -6 to 6
- queries: bfloat16 [32, 2, 384, 4096], P('dp', 'pair', None, 'tensor'), may hold values from -6 to 6
- key_states: bfloat16 [32, 2, 384, 512], P('dp', 'pair', None, 'tensor'), may hold values from -6 to 6
- value_states: bfloat16 [32, 2, 384, 512], P('dp', 'pair', None, 'tensor'), may hold values from -6 to 6
- out_weight: bfloat16 [4096, 2560], P('tensor', ('pair', 'dp')), may hold values from -0.09375 to 0.09375
- norm_gain: float32 [2560], replicated, may hold values from 0.25 to 1.75
- reward_head: float32 [2560], replicated, may hold values from -0.118585412 to 0.118585412
- lengths: int32 [32, 2], P('dp'), may hold values from 96 to 384, as said below
- labels: int32 [32], P('dp'), may hold values from 0 to 1
Outputs:
- layer_out: bfloat16 [32, 2, 384, 2560], P('dp', 'pair', 'tensor')
- pair_loss: float32 [32], P('dp')
- grad_queries: bfloat16 [32, 2, 384, 4096], P('dp', 'pair', None, 'tensor')
- grad_keys: bfloat16 [32, 2, 384, 512], P('dp', 'pair', None, 'tensor')
- grad_values: bfloat16 [32, 2, 384, 512], P('dp', 'pair', None, 'tensor')
- grad_out_weight: float32 [4096, 2560], P('tensor', ('pair', 'dp'))
The draws below stay inside these ranges and needn't reach their ends.
Inputs may be any that keep to these rules, and one draw needn't show every extreme that they name: `lengths`: every response has at least 96 valid tokens; some response fills all 384 in every draw.
All inputs are finite; a program needn't handle non-finite values.
Results may differ from the reference program's by a relative error of at most 0.022.
Values may be sent and summed in bfloat16 or wider, within the bound.
A program may use at most 128 MiB of HBM per device.

```python
import jax
import jax.numpy as jnp
from jax import lax

D = 2560
HEADS = 32
KV_HEADS = 4
HEAD_DIM = 128
TOK = 384
COMPS = 32


def head_factors(key):
    gain_normal = jax.random.normal(jax.random.fold_in(key, 201), (D,), jnp.float32)
    head_normal = jax.random.normal(jax.random.fold_in(key, 203), (D,), jnp.float32)
    return (gain_normal, head_normal)


def draw_norm_gain(key, part):
    gain_normal, head_normal = head_factors(key)
    result = 1.0 + 0.15 * jnp.clip(gain_normal, -5.0, 5.0)
    return result.astype(jnp.float32)


def draw_reward_head(key, part):
    gain_normal, head_normal = head_factors(key)
    result = jnp.clip(head_normal, -6.0, 6.0) * D ** (-0.5)
    return result.astype(jnp.float32)


def draw_hidden_in(key, part):
    key = jax.random.fold_in(key, 13)
    extent = (COMPS, 2, TOK, D)
    result = jnp.clip(jax.random.normal(key, extent, jnp.float32), -6.0, 6.0)
    return result.astype(jnp.bfloat16)


def draw_key_states(key, part):
    key = jax.random.fold_in(key, 7)
    shape = (COMPS, 2, TOK, KV_HEADS, HEAD_DIM)
    base = jnp.clip(jax.random.normal(key, shape, jnp.float32), -6.0, 6.0)
    return base.reshape(COMPS, 2, TOK, KV_HEADS * HEAD_DIM).astype(jnp.bfloat16)


def draw_queries(key, part):
    key = jax.random.fold_in(key, 9)
    groups = HEADS // KV_HEADS
    shape = (COMPS, 2, TOK, KV_HEADS, groups, HEAD_DIM)
    base = jnp.clip(jax.random.normal(key, shape, jnp.float32), -6.0, 6.0)
    return base.reshape(COMPS, 2, TOK, HEADS * HEAD_DIM).astype(jnp.bfloat16)


def draw_lengths(key, part):
    key = jax.random.fold_in(key, 5)
    drawn = jax.random.randint(key, (COMPS * 2,), TOK // 4, TOK + 1)
    chosen = jax.random.randint(jax.random.fold_in(key, 1), (), 0, COMPS * 2)
    filled = jnp.where(jnp.arange(COMPS * 2) == chosen, TOK, drawn)
    return filled.reshape(COMPS, 2).astype(jnp.int32)


def touch_ends(values, rng, smallest, top_value):
    place = [jax.random.randint(jax.random.fold_in(rng, axis), (), 0, length) for axis, length in enumerate(values.shape)]
    main_axis = values.shape.index(max(values.shape))
    beside = place[:main_axis] + [(place[main_axis] + 1) % values.shape[main_axis]] + place[main_axis + 1:]
    return values.at[tuple(place)].set(smallest).at[tuple(beside)].set(top_value)


def level_of(key, shape, cuts, low, largest):
    def one(position, parts):
        draws = jax.random.uniform(jax.random.fold_in(jax.random.fold_in(key, 6), position), (parts,), jnp.float32, low / len(cuts), largest / len(cuts))
        return jnp.repeat(jnp.exp(draws), shape[position] // parts).reshape((-1,) + (1,) * (len(shape) - position - 1))

    factor_of = one(*cuts[0])
    for cut in cuts[1:]:
        factor_of = factor_of * one(*cut)
    return factor_of


def centred(rng, shape, spread, most, cuts=(), held_as=jnp.bfloat16):
    values = jax.random.normal(rng, shape, jnp.float32) * spread
    if len(cuts) > 0:
        values = level_of(rng, shape, cuts, -0.22, 0.18) * values
    return jnp.clip(values, min=-most, max=most).astype(held_as)


def setup_inputs(seed: int = 0) -> dict:
    arg_keys = jax.random.split(jax.random.key(seed), 10)
    return {
        "hidden_in": draw_hidden_in(jax.random.fold_in(arg_keys[9], 71), 0),
        "queries": draw_queries(jax.random.fold_in(arg_keys[9], 71), 0),
        "key_states": draw_key_states(jax.random.fold_in(arg_keys[9], 71), 0),
        "value_states": centred(arg_keys[3], (COMPS, 2, TOK, KV_HEADS * HEAD_DIM), 1.0, 6.0, ((0, 32), (1, 2), (3, 4))),
        "out_weight": centred(arg_keys[4], (HEADS * HEAD_DIM, D), (HEADS * HEAD_DIM) ** -0.5, 0.09375, ((0, 4), (1, 64))),
        "norm_gain": draw_norm_gain(jax.random.fold_in(arg_keys[9], 71), 0),
        "reward_head": draw_reward_head(jax.random.fold_in(arg_keys[9], 71), 0),
        "lengths": draw_lengths(jax.random.fold_in(arg_keys[9], 71), 0),
        "labels": touch_ends(jax.random.randint(arg_keys[8], (COMPS,), 0, 2), jax.random.fold_in(arg_keys[8], 1), 0, 1).astype(jnp.int32),
    }


loss_scale = 1024.0
norm_eps = 1e-06

def visible(len_own, len_par):
    row_ids = jnp.arange(TOK, dtype=jnp.int32)[:, None]
    col_ids = jnp.arange(TOK, dtype=jnp.int32)[None, :]
    own_seen = (col_ids <= row_ids) & (col_ids < len_own)
    par_seen = jnp.broadcast_to(col_ids < len_par, (TOK, TOK))
    return jnp.concatenate([own_seen, par_seen], axis=1)

def probability(query_rows, key_all, allowed):
    scores = jnp.einsum('tkgd,skd->kgts', query_rows.astype(jnp.float32), key_all.astype(jnp.float32)) * HEAD_DIM ** (-0.5)
    scores = jnp.where(allowed, scores, -1e+30)
    row_max = lax.optimization_barrier(jnp.max(scores, axis=-1, keepdims=True))
    exponent = jnp.where(allowed, jnp.exp(scores - row_max), 0.0)
    return exponent / lax.optimization_barrier(jnp.sum(exponent, axis=-1, keepdims=True))

def reference(hidden_in, queries, key_states, value_states, out_weight, norm_gain, reward_head, lengths, labels):
    responses = COMPS * 2
    groups = HEADS // KV_HEADS
    width_heads = HEADS * HEAD_DIM
    query_flat = queries.reshape(responses, TOK, KV_HEADS, groups, HEAD_DIM)
    key_both = jnp.concatenate([key_states, key_states[:, ::-1]], axis=2).reshape(responses, 2 * TOK, KV_HEADS, HEAD_DIM)
    value_both = jnp.concatenate([value_states, value_states[:, ::-1]], axis=2).reshape(responses, 2 * TOK, KV_HEADS, HEAD_DIM)
    len_own = lengths.reshape(responses)
    len_par = lengths[:, ::-1].reshape(responses)

    def forward_one(pieces):
        query_rows, key_all, value_all, own_len, par_len = pieces
        weights = probability(query_rows, key_all, visible(own_len, par_len)).astype(jnp.bfloat16)
        mixed_out = jnp.einsum('kgts,skd->tkgd', weights.astype(jnp.float32), value_all.astype(jnp.float32))
        return mixed_out.reshape(TOK, width_heads).astype(jnp.bfloat16)
    attended = lax.map(forward_one, (query_flat, key_both, value_both, len_own, len_par))
    att_rows = attended.reshape(responses * TOK, width_heads)
    projected = jnp.dot(att_rows, out_weight, preferred_element_type=jnp.float32)
    layer_rows = (hidden_in.reshape(responses * TOK, D).astype(jnp.float32) + projected).astype(jnp.bfloat16)
    layer_f32 = layer_rows.astype(jnp.float32)
    inv_rms = lax.rsqrt(lax.optimization_barrier(jnp.mean(layer_f32 * layer_f32, axis=-1, keepdims=True)) + norm_eps)
    token_score = lax.optimization_barrier(jnp.sum(layer_f32 * inv_rms * norm_gain * reward_head, axis=-1)).reshape(COMPS, 2, TOK)
    positions = jnp.arange(TOK, dtype=jnp.int32)
    valid_rows = (positions[None, None, :] < lengths[:, :, None]).astype(jnp.float32)
    len_root = jnp.sqrt(lengths.astype(jnp.float32))
    reward = lax.optimization_barrier(jnp.sum(token_score * valid_rows, axis=-1)) / len_root
    label_sign = 2.0 * labels.astype(jnp.float32) - 1.0
    margin = label_sign * (reward[:, 0] - reward[:, 1])
    pair_loss = jnp.logaddexp(jnp.float32(0.0), -margin)
    first_slope = -label_sign * jax.nn.sigmoid(-margin) * loss_scale
    slope = jnp.stack([first_slope, -first_slope], axis=1)
    token_coef = (slope[:, :, None] * valid_rows / len_root[:, :, None]).reshape(responses * TOK, 1)
    pull = token_coef * (norm_gain * reward_head)
    grad_rows = (inv_rms * pull - layer_f32 * inv_rms ** 3 * lax.optimization_barrier(jnp.sum(layer_f32 * pull, axis=-1, keepdims=True)) / D).astype(jnp.bfloat16)
    grad_att = lax.dot_general(grad_rows, out_weight, (((1,), (1,)), ((), ())), preferred_element_type=jnp.float32).astype(jnp.bfloat16)
    grad_out_weight = lax.dot_general(att_rows, grad_rows, (((0,), (0,)), ((), ())), preferred_element_type=jnp.float32)
    grad_flat = grad_att.reshape(responses, TOK, KV_HEADS, groups, HEAD_DIM)

    def backward_one(pieces):
        query_rows, key_all, value_all, own_len, par_len, grad_here = pieces
        probs = probability(query_rows, key_all, visible(own_len, par_len))
        weights = probs.astype(jnp.bfloat16)
        grad_f = grad_here.astype(jnp.float32)
        dprob = jnp.einsum('tkgd,skd->kgts', grad_f, value_all.astype(jnp.float32))
        row_dot = lax.optimization_barrier(jnp.sum(probs * dprob, axis=-1, keepdims=True))
        grad_scores = (probs * (dprob - row_dot) * HEAD_DIM ** (-0.5)).astype(jnp.bfloat16).astype(jnp.float32)
        grad_query = jnp.einsum('kgts,skd->tkgd', grad_scores, key_all.astype(jnp.float32)).reshape(TOK, width_heads).astype(jnp.bfloat16)
        key_terms = jnp.einsum('kgts,tkgd->skd', grad_scores, query_rows.astype(jnp.float32)).reshape(2 * TOK, KV_HEADS * HEAD_DIM)
        value_terms = jnp.einsum('kgts,tkgd->skd', weights.astype(jnp.float32), grad_f).reshape(2 * TOK, KV_HEADS * HEAD_DIM)
        return (grad_query, key_terms, value_terms)
    grad_query, key_terms, value_terms = lax.map(backward_one, (query_flat, key_both, value_both, len_own, len_par, grad_flat))
    key_terms = key_terms.reshape(COMPS, 2, 2 * TOK, KV_HEADS * HEAD_DIM)
    value_terms = value_terms.reshape(COMPS, 2, 2 * TOK, KV_HEADS * HEAD_DIM)
    grad_keys = (key_terms[:, :, :TOK] + key_terms[:, ::-1, TOK:]).astype(jnp.bfloat16)
    grad_values = (value_terms[:, :, :TOK] + value_terms[:, ::-1, TOK:]).astype(jnp.bfloat16)
    layer_out = layer_rows.reshape(COMPS, 2, TOK, D)
    grad_queries = grad_query.reshape(COMPS, 2, TOK, width_heads)
    return (layer_out, pair_loss, grad_queries, grad_keys, grad_values, grad_out_weight)
```

```python
from types import SimpleNamespace

import jax
import jax.numpy as jnp
from jax import lax
from jax.experimental import pallas as pl
from jax.experimental.pallas import tpu as pltpu
from jax.sharding import PartitionSpec as P

HEAD_DIM = 128
LOSS_SCALE = 1024.0
NORM_EPS = 1e-06
LOG2E = 1.4426950408889634

TOK = 384
WIDTH = 2560
HEADS = 8
NX, NY, NZ = 4, 4, 8
ROWS = TOK // NX
CHUNKS = 4
CW = WIDTH // CHUNKS
BLK = 80
HALF = 512
LA = 384
LB = HALF - LA

MESH = pl.DeviceIdType.MESH
F32 = jnp.float32
BF16 = jnp.bfloat16

NT = (((1,), (1,)), ((), ()))
TN = (((0,), (0,)), ((), ()))
NN = (((1,), (0,)), ((), ()))


def mm(a, b, dims):
    return lax.dot_general(a, b, dims, preferred_element_type=F32)


def device(x, y, z, c):
    return (z // 4, x, y * 8 + lax.rem(z, 4) * 2 + c)


def rcopy(src, dst, send, recv, dev):
    return pltpu.make_async_remote_copy(
        src_ref=src, dst_ref=dst, send_sem=send, recv_sem=recv, device_id=dev, device_id_type=MESH
    )


DMA = pltpu.SemaphoreType.DMA
ARGS = (
    "lens",
    "labels",
    "hidden",
    "q",
    "k",
    "v",
    "wt",
    "gain",
    "head",
    "layer_o",
    "loss_o",
    "dq_o",
    "dk_o",
    "dv_o",
    "gw_o",
)
SCRATCH = dict(
    wh=pltpu.VMEM((2, 2, NY, 4, BLK, HALF), BF16),
    wf=pltpu.VMEM((2, 40, HALF), F32),
    qv=pltpu.VMEM((TOK, HEADS * HEAD_DIM), BF16),
    hv=pltpu.VMEM((ROWS, WIDTH), BF16),
    lv=pltpu.VMEM((ROWS, WIDTH), BF16),
    dqv=pltpu.VMEM((TOK, HEADS * HEAD_DIM), BF16),
    asm=pltpu.VMEM((BLK, HALF), F32),
    kall=pltpu.VMEM((2 * TOK, HEAD_DIM), BF16),
    vall=pltpu.VMEM((2 * TOK, HEAD_DIM), BF16),
    ktr=pltpu.VMEM((HEAD_DIM, 2 * TOK), BF16),
    vtr=pltpu.VMEM((HEAD_DIM, 2 * TOK), BF16),
    bias=pltpu.VMEM((2 * TOK, TOK), F32),
    lse=pltpu.VMEM((HEADS, 1, TOK), F32),
    att=pltpu.VMEM((2, TOK, HALF), BF16),
    acc=pltpu.VMEM((CHUNKS, NX, ROWS, CW), F32),
    xs=pltpu.VMEM((CHUNKS, NX, ROWS, CW), BF16),
    xr=pltpu.VMEM((3, CHUNKS, ROWS, CW), BF16),
    gf=pltpu.VMEM((CHUNKS, NX, ROWS, CW), BF16),
    rw=pltpu.VMEM((2, NX, 8, 128), F32),
    own=pltpu.VMEM((CHUNKS, CW, HALF), F32),
    mo=pltpu.VMEM((CHUNKS, CW, HALF), BF16),
    mi=pltpu.VMEM((CHUNKS, CW, HALF), BF16),
    red=pltpu.VMEM((2, NY, 4, BLK, HALF), BF16),
    yl=pltpu.VMEM((3, 2, 4, BLK, LA), BF16),
    zsend=pltpu.VMEM((2, 4, BLK, LA), BF16),
    zl=pltpu.VMEM((7, BLK, LA), BF16),
    z2l=pltpu.VMEM((7, 2, 2, BLK, LB), BF16),
    y2send=pltpu.VMEM((NY, BLK, LB), BF16),
    y2l=pltpu.VMEM((3, BLK, LB), BF16),
    gwc=pltpu.VMEM((BLK, HALF), F32),
    gwr=pltpu.VMEM((40, HALF), F32),
    gacc=pltpu.VMEM((2, TOK, HALF), F32),
    gatt=pltpu.VMEM((2, TOK, HALF), BF16),
    dk=pltpu.VMEM((2 * TOK, HEAD_DIM), F32),
    dv=pltpu.VMEM((2 * TOK, HEAD_DIM), F32),
    dkv_out=pltpu.VMEM((2, TOK, HEAD_DIM), BF16),
    dkv_in=pltpu.VMEM((2, TOK, HEAD_DIM), BF16),
    s_kv=DMA((4,)),
    r_kv=DMA((4,)),
    s_c=DMA((4,)),
    r_c=DMA((4,)),
    s_z=DMA((7,)),
    r_z=DMA((7,)),
    s_y=DMA((3, 8)),
    r_y=DMA((3, 8)),
    s_z2=DMA((7,)),
    r_z2=DMA((7,)),
    s_x=DMA((3, CHUNKS)),
    r_x=DMA((3, CHUNKS)),
    s_g=DMA((3, CHUNKS)),
    r_g=DMA((3, CHUNKS)),
    s_rw=DMA((7,)),
    r_rw=DMA((7,)),
    s_m=DMA((CHUNKS,)),
    r_m=DMA((CHUNKS,)),
    t_z=DMA((7,)),
    u_z=DMA((7,)),
    t_y=DMA((3, 2)),
    u_y=DMA((3, 2)),
    t_z2=DMA((7, 2)),
    u_z2=DMA((7, 2)),
    loc=DMA((8,)),
    out_l=DMA((CHUNKS,)),
    out_q=DMA((HEADS,)),
    t_y2=DMA((3,)),
    u_y2=DMA((3,)),
)


def kernel(*refs):
    names = SimpleNamespace(**dict(zip(ARGS + tuple(SCRATCH), refs)))
    run(names)


def run(n):
    lens = n.lens
    labels = n.labels
    hidden = n.hidden
    q = n.q
    k = n.k
    v = n.v
    wt = n.wt
    gain = n.gain
    head = n.head
    layer_o = n.layer_o
    loss_o = n.loss_o
    dq_o = n.dq_o
    dk_o = n.dk_o
    dv_o = n.dv_o
    gw_o = n.gw_o
    wh = n.wh
    wf = n.wf
    qv = n.qv
    hv = n.hv
    lv = n.lv
    dqv = n.dqv
    asm = n.asm
    kall = n.kall
    vall = n.vall
    ktr = n.ktr
    vtr = n.vtr
    bias = n.bias
    lse = n.lse
    att = n.att
    acc = n.acc
    xs = n.xs
    xr = n.xr
    gf = n.gf
    rw = n.rw
    own = n.own
    mo = n.mo
    mi = n.mi
    red = n.red
    yl = n.yl
    zsend = n.zsend
    zl = n.zl
    z2l = n.z2l
    y2send = n.y2send
    y2l = n.y2l
    gwc = n.gwc
    gwr = n.gwr
    gacc = n.gacc
    gatt = n.gatt
    dk = n.dk
    dv = n.dv
    dkv_out = n.dkv_out
    dkv_in = n.dkv_in
    s_kv = n.s_kv
    r_kv = n.r_kv
    s_c = n.s_c
    r_c = n.r_c
    s_z = n.s_z
    r_z = n.r_z
    s_y = n.s_y
    r_y = n.r_y
    s_z2 = n.s_z2
    r_z2 = n.r_z2
    s_x = n.s_x
    r_x = n.r_x
    s_g = n.s_g
    r_g = n.r_g
    s_rw = n.s_rw
    r_rw = n.r_rw
    s_m = n.s_m
    r_m = n.r_m
    t_z = n.t_z
    u_z = n.u_z
    t_y = n.t_y
    u_y = n.u_y
    t_z2 = n.t_z2
    u_z2 = n.u_z2
    loc = n.loc
    out_l = n.out_l
    out_q = n.out_q
    t_y2 = n.t_y2
    u_y2 = n.u_y2

    pair = lax.axis_index("pair")
    x = lax.axis_index("tensor")
    dp = lax.axis_index("dp")
    y = dp // 8
    zlo = lax.rem(dp // 2, 4)
    z = pair * 4 + zlo
    c = lax.rem(dp, 2)
    mate = 1 - c

    def xdev(d):
        return device(lax.rem(x + d, NX), y, z, c)

    def ydev(d):
        return device(x, lax.rem(y + d, NY), z, c)

    def zdev(d):
        return device(x, y, lax.rem(z + d, NZ), c)

    core = device(x, y, z, mate)
    far = zdev(4)

    def rwdev(i):
        dpair, dx = i // 4, i % 4
        return device(lax.rem(x + dx, NX), y, lax.rem(z + 4 * dpair, NZ), c)

    local = [
        pltpu.make_async_copy(k, kall.at[pl.ds(0, TOK)], loc.at[0]),
        pltpu.make_async_copy(v, vall.at[pl.ds(0, TOK)], loc.at[1]),
        pltpu.make_async_copy(q, qv, loc.at[2]),
    ]
    load_hidden = pltpu.make_async_copy(hidden, hv, loc.at[3])
    for cp in local + [load_hidden]:
        cp.start()

    barrier = pltpu.get_barrier_semaphore()
    peers = [core]
    peers += [rwdev(i) for i in range(1, 8)]
    peers += [ydev(d) for d in (1, 2, 3)]
    peers += [zdev(d) for d in (1, 2, 3, 5, 6, 7)]
    for peer in peers:
        pl.semaphore_signal(barrier, inc=1, device_id=peer, device_id_type=MESH)

    len_own = jnp.where(pair == 0, lens[0, 0], lens[0, 1])
    len_par = jnp.where(pair == 0, lens[0, 1], lens[0, 0])
    key_id = lax.broadcasted_iota(jnp.int32, (TOK, TOK), 0)
    tok_id = lax.broadcasted_iota(jnp.int32, (TOK, TOK), 1)
    bias[0:TOK, :] = jnp.where((key_id <= tok_id) & (key_id < len_own), 0.0, -1e30)
    bias[TOK:, :] = jnp.where(key_id < len_par, 0.0, -1e30)

    for half in range(2):
        wf[half] = wt[:, pl.ds(half * HALF, HALF)].astype(F32)

    pl.semaphore_wait(barrier, len(peers))

    kv_copies = [
        rcopy(k, kall.at[pl.ds(TOK, TOK)], s_kv.at[0], r_kv.at[0], far),
        rcopy(v, vall.at[pl.ds(TOK, TOK)], s_kv.at[1], r_kv.at[1], far),
    ]
    mine = pl.ds(pl.multiple_of(c * 40, 8), 40)
    wcore = rcopy(wf.at[mate], asm.at[mine], s_c.at[0], r_c.at[0], core)
    wcore.start()
    for cp in kv_copies:
        cp.start()

    asm[mine, :] = wf[c]
    wcore.wait()
    wh[c, pair, y, zlo] = asm[...].astype(BF16)

    own_all = wh.at[c, pair, y, zlo]
    own_a = wh.at[c, pair, y, zlo, :, pl.ds(0, LA)]
    y0 = [rcopy(own_all, own_all, s_y.at[d - 1, 0], r_y.at[d - 1, 0], ydev(d)) for d in range(1, NY)]

    def hop(e):
        there = lax.rem(pair + e // 4, 2) * 4 + lax.rem(zlo + e, 4)
        return there, lax.rem(there - z + NZ, NZ)

    def za_copy(d):
        return rcopy(own_a, own_a, s_z.at[d - 1], r_z.at[d - 1], zdev(d))

    for cp in y0:
        cp.start()
    for e in range(1, 8):
        za_copy(hop(e)[1]).start()

    for cp in y0:
        cp.wait()
    part_b = wh.at[c, pair, :, zlo, :, pl.ds(LA, LB)]

    def zb_copy(d):
        return rcopy(part_b, part_b, s_z2.at[d - 1], r_z2.at[d - 1], zdev(d))

    for e in range(1, 8):
        zb_copy(hop(e)[1]).start()

    for cp in local + kv_copies:
        cp.wait()
    ktr[...] = jnp.transpose(kall[...].astype(F32)).astype(BF16)
    vtr[...] = jnp.transpose(vall[...].astype(F32)).astype(BF16)

    def ya_copy(e, d):
        there, _ = hop(e)
        part = wh.at[c, there // 4, y, lax.rem(there, 4), :, pl.ds(0, LA)]
        return rcopy(part, part, s_y.at[d - 1, e], r_y.at[d - 1, e], ydev(d))

    scale2 = HEAD_DIM ** (-0.5) * LOG2E

    def forward(h, carry):
        cols = pl.ds(pl.multiple_of(h * HEAD_DIM, HEAD_DIM), HEAD_DIM)
        s = mm(kall[...], qv[:, cols], NT) * scale2 + bias[...]
        top = jnp.max(s, axis=0, keepdims=True)
        e = jnp.exp2(s - top)
        total = jnp.sum(e, axis=0, keepdims=True)
        out = mm(vtr[...], e.astype(BF16), NN) * (1.0 / total)
        lane = pl.ds(pl.multiple_of(lax.rem(h, 4) * HEAD_DIM, HEAD_DIM), HEAD_DIM)
        att[h // 4, :, lane] = jnp.transpose(out).astype(BF16)
        lse[h] = top + jnp.log2(total)
        return carry

    def forward_relay(h, carry):
        forward(h, carry)
        e = h + 1
        _, there = hop(e)
        za_copy(NZ - there).wait_recv()
        for d in (2, 1, 3):
            ya_copy(e, d).start()
        return carry

    lax.fori_loop(0, HEADS - 1, forward_relay, 0)
    forward(HEADS - 1, 0)

    def wrows(half, j):
        return wh[half, j // 2, pl.ds(lax.rem(j, 2) * 2, 2)].reshape(CW, HALF)

    def project_own(i, carry):
        j = lax.rem(i + 2 * pair, CHUNKS)
        acc[j] = mm(att[c], wrows(c, j), NT).reshape(NX, ROWS, CW)
        return carry

    def xcopy(d, j):
        return rcopy(
            xs.at[j, lax.rem(x + d, NX)], xr.at[d - 1, j], s_x.at[d - 1, j], r_x.at[d - 1, j], xdev(d)
        )

    def project_rest(i, carry):
        j = lax.rem(i + 2 * pair, CHUNKS)
        p = acc[j] + mm(att[mate], wrows(mate, j), NT).reshape(NX, ROWS, CW)
        acc[j] = p
        xs[j] = p.astype(BF16)
        for d in (2, 1, 3):
            xcopy(d, j).start()
        return carry

    for part in range(2):
        for e in range(4 * part, 4 * part + 4):
            if e > 0:
                zb_copy(NZ - hop(e)[1]).wait_recv()
                for d in (1, 2, 3):
                    ya_copy(e, d).wait_recv()
        zh = lax.rem(pair + part, 2)
        swap = rcopy(wh.at[c, zh], wh.at[c, zh], s_c.at[1 + part], r_c.at[1 + part], core)
        swap.start()
        lax.fori_loop(2 * part, 2 * part + 2, project_own, 0)
        swap.wait()
        lax.fori_loop(2 * part, 2 * part + 2, project_rest, 0)
    for e in range(1, 8):
        za_copy(e).wait_send()
        zb_copy(e).wait_send()
        for d in (1, 2, 3):
            ya_copy(e, d).wait_send()
    load_hidden.wait()

    def layer_copy(j):
        cols = pl.ds(pl.multiple_of(j * CW, 128), CW)
        return pltpu.make_async_copy(lv.at[:, cols], layer_o.at[:, cols], out_l.at[j])

    def layer(i, carry):
        square, along = carry
        j = lax.rem(i + 2 * pair, CHUNKS)
        for d in (1, 2, 3):
            xcopy(d, j).wait()
        cols = pl.ds(pl.multiple_of(j * CW, 128), CW)
        total = hv[:, cols].astype(F32) + acc[j, x]
        for d in (1, 2, 3):
            total += xr[d - 1, j].astype(F32)
        rounded = total.astype(BF16)
        lv[:, cols] = rounded
        layer_copy(j).start()
        value = rounded.astype(F32)
        factor = gain[:, cols] * head[:, cols]
        square += jnp.sum(value * value, axis=1, keepdims=True)
        along += jnp.sum(value * factor, axis=1, keepdims=True)
        return square, along

    zero = jnp.zeros((ROWS, 1), F32)
    square, along = lax.fori_loop(0, CHUNKS, layer, (zero, zero))
    inv = lax.rsqrt(square * (1.0 / WIDTH) + NORM_EPS)
    position = x * ROWS + lax.broadcasted_iota(jnp.int32, (ROWS, 1), 0)
    valid = jnp.where(position < len_own, 1.0, 0.0)
    root = jnp.sqrt(jnp.full((ROWS, 1), len_own, jnp.int32).astype(F32))
    weight = valid / root
    partial = jnp.sum(inv * along * weight, axis=0, keepdims=True)
    rw[pair, x] = jnp.broadcast_to(partial, (8, 128))
    own_rw = rw.at[pair, x]
    rw_copies = [rcopy(own_rw, own_rw, s_rw.at[i - 1], r_rw.at[i - 1], rwdev(i)) for i in range(1, 8)]
    for cp in rw_copies:
        cp.start()

    gscale = inv * weight
    gcorr = inv * inv * inv * along * weight * (1.0 / WIDTH)

    def gcopy(d, j):
        own = gf.at[j, x]
        return rcopy(own, own, s_g.at[d - 1, j], r_g.at[d - 1, j], xdev(d))

    def rows_grad(i, carry):
        j = lax.rem(i + 2 * pair, CHUNKS)
        cols = pl.ds(pl.multiple_of(j * CW, 128), CW)
        factor = gain[:, cols] * head[:, cols]
        value = lv[:, cols].astype(F32)
        gf[j, x] = (gscale * factor - value * gcorr).astype(BF16)
        for d in (2, 1, 3):
            gcopy(d, j).start()
        return carry

    lax.fori_loop(0, CHUNKS, rows_grad, 0)

    for cp in rw_copies:
        cp.wait()
    reward0 = rw[0, 0] + rw[0, 1] + rw[0, 2] + rw[0, 3]
    reward1 = rw[1, 0] + rw[1, 1] + rw[1, 2] + rw[1, 3]
    sign = 2.0 * jnp.full((8, 128), labels[0], jnp.int32).astype(F32) - 1.0
    margin = sign * (reward0 - reward1)
    loss_o[...] = jnp.maximum(-margin, 0.0) + jnp.log1p(jnp.exp(-jnp.abs(margin)))
    first = -sign * jax.nn.sigmoid(-margin) * LOSS_SCALE
    side = jnp.where(pair == 0, 1.0, -1.0)
    slope = (first * side)[0:1, 0:1]

    def mcopy(j):
        return rcopy(mo.at[j], mi.at[j], s_m.at[j], r_m.at[j], core)

    gacc[...] = jnp.zeros_like(gacc)

    def products(i):
        j = lax.rem(i + 2 * pair, CHUNKS)
        for d in (1, 2, 3):
            gcopy(d, j).wait()
        g = gf[j].reshape(TOK, CW)
        mo[j] = (mm(g, att[mate], TN) * slope).astype(BF16)
        mcopy(j).start()
        own[j] = mm(g, att[c], TN) * slope
        for half in range(2):
            gacc[half] += mm(g, wrows(half, j), NN)

    def ycopy2(d, zh):
        src = red.at[zh, lax.rem(y + d, NY), :, :, pl.ds(0, LA)]
        return rcopy(src, yl.at[d - 1, zh], t_y.at[d - 1, zh], u_y.at[d - 1, zh], ydev(d))

    def zcopy2(d, yp):
        to = lax.rem(z + d, NZ)
        src = red.at[to // 4, pl.ds(2 * yp, 2), lax.rem(to, 4), :, pl.ds(LA, LB)]
        return rcopy(src, z2l.at[d - 1, yp], t_z2.at[d - 1, yp], u_z2.at[d - 1, yp], zdev(d))

    def merge(i):
        j = lax.rem(i + 2 * pair, CHUNKS)
        zh = j // 2
        yp = lax.rem(j, 2)
        mcopy(j).wait()
        both = own[j] + mi[j].astype(F32)
        red[zh, pl.ds(yp * 2, 2)] = both.astype(BF16).reshape(2, 4, BLK, HALF)
        for d in (2, 1, 3):
            @pl.when(lax.rem(y + d, NY) // 2 == yp)
            def _():
                ycopy2(d, zh).start()
        for d in (4, 3, 5, 2, 6, 1, 7):
            @pl.when(lax.rem(z + d, NZ) // 4 == zh)
            def _():
                zcopy2(d, yp).start()

    def step(i, carry):
        products(i)
        merge(i - 1)
        return carry

    products(0)
    lax.fori_loop(1, CHUNKS, step, 0)
    merge(CHUNKS - 1)

    gatt[...] = gacc[...].astype(BF16)
    dk[...] = jnp.zeros_like(dk)
    dv[...] = jnp.zeros_like(dv)
    slope_scaled = slope * HEAD_DIM ** (-0.5)

    def dq_copy(h):
        cols = pl.ds(pl.multiple_of(h * HEAD_DIM, HEAD_DIM), HEAD_DIM)
        return pltpu.make_async_copy(dqv.at[:, cols], dq_o.at[:, cols], out_q.at[h])

    def backward(h, carry):
        cols = pl.ds(pl.multiple_of(h * HEAD_DIM, HEAD_DIM), HEAD_DIM)
        lane = pl.ds(pl.multiple_of(lax.rem(h, 4) * HEAD_DIM, HEAD_DIM), HEAD_DIM)
        qh = qv[:, cols]
        gh = gatt[h // 4, :, lane]
        p = jnp.exp2(mm(kall[...], qh, NT) * scale2 + bias[...] - lse[h])
        dprob = mm(vall[...], gh, NT)
        delta = jnp.sum(p * dprob, axis=0, keepdims=True)
        ds = (p * (dprob - delta)).astype(BF16)
        dv[...] += mm(p.astype(BF16), gh, NN)
        dk[...] += mm(ds, qh, NN)
        dqv[:, cols] = (jnp.transpose(mm(ktr[...], ds, NN)) * slope_scaled).astype(BF16)
        dq_copy(h).start()
        return carry

    def zcopy1(d):
        to = lax.rem(z + d, NZ)
        src = zsend.at[to // 4, lax.rem(to, 4)]
        return rcopy(src, zl.at[d - 1], t_z.at[d - 1], u_z.at[d - 1], zdev(d))

    def ysum(part):
        zh = lax.rem(pair + part, 2)
        total = red[zh, y, :, :, pl.ds(0, LA)].astype(F32)
        for d in (1, 2, 3):
            ycopy2(d, zh).wait_recv()
            total += yl[d - 1, zh].astype(F32)
        zsend[zh] = total.astype(BF16)
        for e in range(4 * part, 4 * part + 4):
            if e > 0:
                zcopy1(hop(e)[1]).start()

    lax.fori_loop(0, 2, backward, 0)
    ysum(0)
    lax.fori_loop(2, 5, backward, 0)
    ysum(1)
    lax.fori_loop(5, HEADS, backward, 0)

    dkv_out[0] = (dk[TOK:, :] * slope_scaled).astype(BF16)
    dkv_out[1] = (dv[TOK:, :] * slope).astype(BF16)
    back = [rcopy(dkv_out.at[i], dkv_in.at[i], s_kv.at[2 + i], r_kv.at[2 + i], far) for i in range(2)]
    for cp in back:
        cp.start()

    part = red[pair, :, zlo, :, pl.ds(LA, LB)].astype(F32).reshape(2, 2, BLK, LB)
    for d in range(1, 8):
        for yp in range(2):
            zcopy2(d, yp).wait()
        part += z2l[d - 1].astype(F32)
    y2send[...] = part.astype(BF16).reshape(NY, BLK, LB)
    yb2 = []
    for d in (2, 1, 3):
        src = y2send.at[lax.rem(y + d, NY)]
        yb2.append(rcopy(src, y2l.at[d - 1], t_y2.at[d - 1], u_y2.at[d - 1], ydev(d)))
        yb2[-1].start()
    for d in range(1, 8):
        zcopy1(d).wait()
    for d in (1, 2, 3):
        for zh in range(2):
            ycopy2(d, zh).wait_send()
    part = zsend[pair, zlo].astype(F32)
    for d in range(7):
        part += zl[d].astype(F32)
    gwc[:, 0:LA] = part
    for cp in yb2:
        cp.wait()
    part = y2send[y].astype(F32)
    for d in range(3):
        part += y2l[d].astype(F32)
    gwc[:, LA:] = part
    mate_rows = gwc.at[pl.ds(pl.multiple_of(mate * 40, 8), 40)]
    gswap = rcopy(mate_rows, gwr, s_c.at[3], r_c.at[3], core)
    gswap.start()
    gw_o[:, pl.ds(pl.multiple_of(c * HALF, HALF), HALF)] = gwc[mine, :]
    gswap.wait()
    gw_o[:, pl.ds(pl.multiple_of(mate * HALF, HALF), HALF)] = gwr[...]

    for j in range(CHUNKS):
        layer_copy(j).wait()
    for h in range(HEADS):
        dq_copy(h).wait()
    for cp in back:
        cp.wait()
    dk_o[...] = (dk[0:TOK, :] * slope_scaled + dkv_in[0].astype(F32)).astype(BF16)
    dv_o[...] = (dv[0:TOK, :] * slope + dkv_in[1].astype(F32)).astype(BF16)


def per_device(hidden_in, queries, key_states, value_states, out_weight, norm_gain, reward_head, lengths, labels):
    smem = pl.BlockSpec(memory_space=pltpu.SMEM)
    vmem = pl.BlockSpec(memory_space=pltpu.VMEM)
    hbm = pl.BlockSpec(memory_space=pl.ANY)
    layer_rows, loss, grad_query, grad_keys, grad_values, grad_weight = pl.pallas_call(
        kernel,
        out_shape=(
            jax.ShapeDtypeStruct((ROWS, WIDTH), BF16),
            jax.ShapeDtypeStruct((8, 128), F32),
            jax.ShapeDtypeStruct((TOK, HEADS * HEAD_DIM), BF16),
            jax.ShapeDtypeStruct((TOK, HEAD_DIM), BF16),
            jax.ShapeDtypeStruct((TOK, HEAD_DIM), BF16),
            jax.ShapeDtypeStruct((40, 2 * HALF), F32),
        ),
        in_specs=[smem, smem] + [hbm] * 4 + [vmem] * 3,
        out_specs=(hbm, vmem, hbm, vmem, vmem, vmem),
        scratch_shapes=list(SCRATCH.values()),
        compiler_params=pltpu.CompilerParams(
            collective_id=0, has_side_effects=True, vmem_limit_bytes=60 * 2**20
        ),
        cost_estimate=pl.CostEstimate(flops=12 * 10**9, bytes_accessed=10 * 2**20, transcendentals=0),
    )(
        lengths,
        labels,
        hidden_in[0, 0],
        queries[0, 0],
        key_states[0, 0],
        value_states[0, 0],
        out_weight.T,
        norm_gain[None],
        reward_head[None],
    )
    return (
        layer_rows[None, None],
        loss[0, 0:1],
        grad_query[None, None],
        grad_keys[None, None],
        grad_values[None, None],
        grad_weight.T,
    )


def solution(mesh):
    in_specs = (
        P("dp", "pair", "tensor", None),
        P("dp", "pair", None, "tensor"),
        P("dp", "pair", None, "tensor"),
        P("dp", "pair", None, "tensor"),
        P("tensor", ("pair", "dp")),
        P(),
        P(),
        P("dp", None),
        P("dp"),
    )
    out_specs = (
        P("dp", "pair", "tensor", None),
        P("dp"),
        P("dp", "pair", None, "tensor"),
        P("dp", "pair", None, "tensor"),
        P("dp", "pair", None, "tensor"),
        P("tensor", ("pair", "dp")),
    )
    return jax.shard_map(
        per_device, mesh=mesh, in_specs=in_specs, out_specs=out_specs, check_vma=False
    )
```

```python
from types import SimpleNamespace

import jax
import jax.numpy as jnp
from jax import lax
from jax.experimental import pallas as pl
from jax.experimental.pallas import tpu as pltpu
from jax.sharding import PartitionSpec as P

HEAD_DIM = 128
LOSS_SCALE = 1024.0
NORM_EPS = 1e-06
LOG2E = 1.4426950408889634

TOK = 384
WIDTH = 2560
HEADS = 8
NX, NY, NZ = 4, 4, 8
ROWS = TOK // NX
CHUNKS = 4
CW = WIDTH // CHUNKS
BLK = 80
HALF = 512
HR = ROWS // 2
HL = HALF // 2
LA = 384
LB = HALF - LA

MESH = pl.DeviceIdType.MESH
F32 = jnp.float32
BF16 = jnp.bfloat16

NT = (((1,), (1,)), ((), ()))
TN = (((0,), (0,)), ((), ()))
NN = (((1,), (0,)), ((), ()))


def mm(a, b, dims):
    return lax.dot_general(a, b, dims, preferred_element_type=F32)


def device(x, y, z, c):
    return (z // 4, x, y * 8 + lax.rem(z, 4) * 2 + c)


def rcopy(src, dst, send, recv, dev):
    return pltpu.make_async_remote_copy(
        src_ref=src, dst_ref=dst, send_sem=send, recv_sem=recv, device_id=dev, device_id_type=MESH
    )


DMA = pltpu.SemaphoreType.DMA
ARGS = (
    "lens",
    "labels",
    "hidden",
    "q",
    "k",
    "v",
    "wt",
    "gain",
    "head",
    "layer_o",
    "loss_o",
    "dq_o",
    "dk_o",
    "dv_o",
    "gw_o",
)
SCRATCH = dict(
    wh=pltpu.VMEM((2, 2, NY, 4, BLK, HALF), BF16),
    wf=pltpu.VMEM((2, 40, HALF), F32),
    qv=pltpu.VMEM((TOK, HEADS * HEAD_DIM), BF16),
    hv=pltpu.VMEM((ROWS, WIDTH), BF16),
    lv=pltpu.VMEM((ROWS, WIDTH), BF16),
    dqv=pltpu.VMEM((TOK, HEADS * HEAD_DIM), BF16),
    asm=pltpu.VMEM((BLK, HALF), F32),
    kall=pltpu.VMEM((2 * TOK, HEAD_DIM), BF16),
    vall=pltpu.VMEM((2 * TOK, HEAD_DIM), BF16),
    ktr=pltpu.VMEM((HEAD_DIM, 2 * TOK), BF16),
    vtr=pltpu.VMEM((HEAD_DIM, 2 * TOK), BF16),
    bias=pltpu.VMEM((2 * TOK, TOK), F32),
    peak=pltpu.VMEM((HEADS, 1, TOK), F32),
    mass=pltpu.VMEM((HEADS, 1, TOK), F32),
    part_out=pltpu.VMEM((HEADS, HEAD_DIM, TOK), F32),
    lse=pltpu.VMEM((HEADS, 1, TOK), F32),
    att=pltpu.VMEM((2, TOK, HALF), BF16),
    acc=pltpu.VMEM((CHUNKS, NX, ROWS, CW), F32),
    xs=pltpu.VMEM((CHUNKS, NX, ROWS, CW), BF16),
    xin=pltpu.VMEM((2, CHUNKS, ROWS, CW), BF16),
    xrel=pltpu.VMEM((2, CHUNKS, HR, CW), BF16),
    xro=pltpu.VMEM((2, CHUNKS, HR, CW), BF16),
    gf=pltpu.VMEM((CHUNKS, NX, ROWS, CW), BF16),
    rw=pltpu.VMEM((2, NX, 8, 128), F32),
    own=pltpu.VMEM((CHUNKS, CW, HALF), F32),
    mo=pltpu.VMEM((CHUNKS, CW, HALF), BF16),
    mi=pltpu.VMEM((CHUNKS, CW, HALF), BF16),
    red=pltpu.VMEM((2, NY, 4, BLK, HALF), BF16),
    yin=pltpu.VMEM((2, 2, 4, BLK, LA), BF16),
    yrel=pltpu.VMEM((2, 2, 2, BLK, LA), BF16),
    yro=pltpu.VMEM((2, 2, 2, BLK, LA), BF16),
    zsend=pltpu.VMEM((2, 4, BLK, LA), BF16),
    zl=pltpu.VMEM((7, BLK, LA), BF16),
    z2l=pltpu.VMEM((7, 2, 2, BLK, LB), BF16),
    y2send=pltpu.VMEM((NY, BLK, LB), BF16),
    y2l=pltpu.VMEM((3, BLK, LB), BF16),
    factor=pltpu.VMEM((1, WIDTH), F32),
    gwc=pltpu.VMEM((BLK, HALF), F32),
    gwr=pltpu.VMEM((40, HALF), F32),
    gacc=pltpu.VMEM((2, TOK, HALF), F32),
    gatt=pltpu.VMEM((2, TOK, HALF), BF16),
    dk=pltpu.VMEM((2 * TOK, HEAD_DIM), F32),
    dv=pltpu.VMEM((2 * TOK, HEAD_DIM), F32),
    dkv_out=pltpu.VMEM((2, TOK, HEAD_DIM), BF16),
    dkv_in=pltpu.VMEM((2, TOK, HEAD_DIM), BF16),
    s_kv=DMA((4,)),
    r_kv=DMA((4,)),
    s_c=DMA((4,)),
    r_c=DMA((4,)),
    s_z=DMA((8,)),
    r_z=DMA((8,)),
    s_w=DMA((8,)),
    r_w=DMA((8,)),
    s_y=DMA((4, 8)),
    r_y=DMA((4, 8)),
    s_x=DMA((3, 2, CHUNKS)),
    r_x=DMA((3, 2, CHUNKS)),
    s_g=DMA((2, 2, CHUNKS)),
    r_g=DMA((2, 2, CHUNKS)),
    s_rw=DMA((4,)),
    r_rw=DMA((4,)),
    s_m=DMA((CHUNKS,)),
    r_m=DMA((CHUNKS,)),
    t_z=DMA((7,)),
    u_z=DMA((7,)),
    t_y=DMA((3, 2, 2)),
    u_y=DMA((3, 2, 2)),
    t_z2=DMA((7, 2)),
    u_z2=DMA((7, 2)),
    loc=DMA((8,)),
    out_l=DMA((CHUNKS,)),
    out_q=DMA((HEADS,)),
    t_y2=DMA((3,)),
    u_y2=DMA((3,)),
)


def kernel(*refs):
    names = SimpleNamespace(**dict(zip(ARGS + tuple(SCRATCH), refs)))
    run(names)


def run(n):
    lens = n.lens
    labels = n.labels
    hidden = n.hidden
    q = n.q
    k = n.k
    v = n.v
    wt = n.wt
    gain = n.gain
    head = n.head
    layer_o = n.layer_o
    loss_o = n.loss_o
    dq_o = n.dq_o
    dk_o = n.dk_o
    dv_o = n.dv_o
    gw_o = n.gw_o
    wh = n.wh
    wf = n.wf
    qv = n.qv
    hv = n.hv
    lv = n.lv
    dqv = n.dqv
    asm = n.asm
    kall = n.kall
    vall = n.vall
    ktr = n.ktr
    vtr = n.vtr
    bias = n.bias
    peak = n.peak
    mass = n.mass
    part_out = n.part_out
    lse = n.lse
    att = n.att
    acc = n.acc
    xs = n.xs
    xin = n.xin
    xrel = n.xrel
    xro = n.xro
    gf = n.gf
    rw = n.rw
    own = n.own
    mo = n.mo
    mi = n.mi
    red = n.red
    yin = n.yin
    yrel = n.yrel
    yro = n.yro
    zsend = n.zsend
    zl = n.zl
    z2l = n.z2l
    y2send = n.y2send
    y2l = n.y2l
    factor = n.factor
    gwc = n.gwc
    gwr = n.gwr
    gacc = n.gacc
    gatt = n.gatt
    dk = n.dk
    dv = n.dv
    dkv_out = n.dkv_out
    dkv_in = n.dkv_in
    s_kv = n.s_kv
    r_kv = n.r_kv
    s_c = n.s_c
    r_c = n.r_c
    s_z = n.s_z
    r_z = n.r_z
    s_w = n.s_w
    r_w = n.r_w
    s_y = n.s_y
    r_y = n.r_y
    s_x = n.s_x
    r_x = n.r_x
    s_g = n.s_g
    r_g = n.r_g
    s_rw = n.s_rw
    r_rw = n.r_rw
    s_m = n.s_m
    r_m = n.r_m
    t_z = n.t_z
    u_z = n.u_z
    t_y = n.t_y
    u_y = n.u_y
    t_z2 = n.t_z2
    u_z2 = n.u_z2
    loc = n.loc
    out_l = n.out_l
    out_q = n.out_q
    t_y2 = n.t_y2
    u_y2 = n.u_y2

    pair = lax.axis_index("pair")
    x = lax.axis_index("tensor")
    dp = lax.axis_index("dp")
    y = dp // 8
    zlo = lax.rem(dp // 2, 4)
    z = pair * 4 + zlo
    c = lax.rem(dp, 2)
    mate = 1 - c

    def xdev(d):
        return device(lax.rem(x + d, NX), y, z, c)

    def ydev(d):
        return device(x, lax.rem(y + d, NY), z, c)

    def zdev(d):
        return device(x, y, lax.rem(z + d, NZ), c)

    core = device(x, y, z, mate)
    far = zdev(4)

    local = [
        pltpu.make_async_copy(k, kall.at[pl.ds(0, TOK)], loc.at[0]),
        pltpu.make_async_copy(v, vall.at[pl.ds(0, TOK)], loc.at[1]),
        pltpu.make_async_copy(q, qv, loc.at[2]),
    ]
    load_hidden = pltpu.make_async_copy(hidden, hv, loc.at[3])
    for cp in local + [load_hidden]:
        cp.start()

    barrier = pltpu.get_barrier_semaphore()
    peers = [core]
    peers += [xdev(d) for d in (1, 2, 3)]
    peers += [ydev(d) for d in (1, 2, 3)]
    peers += [zdev(d) for d in range(1, NZ)]
    for peer in peers:
        pl.semaphore_signal(barrier, inc=1, device_id=peer, device_id_type=MESH)

    len_own = jnp.where(pair == 0, lens[0, 0], lens[0, 1])
    len_par = jnp.where(pair == 0, lens[0, 1], lens[0, 0])
    key_id = lax.broadcasted_iota(jnp.int32, (TOK, TOK), 0)
    tok_id = lax.broadcasted_iota(jnp.int32, (TOK, TOK), 1)
    bias[0:TOK, :] = jnp.where((key_id <= tok_id) & (key_id < len_own), 0.0, -1e30)
    bias[TOK:, :] = jnp.where(key_id < len_par, 0.0, -1e30)

    for half in range(2):
        wf[half] = wt[:, pl.ds(half * HALF, HALF)].astype(F32)

    factor[...] = (gain[...] * head[...]).reshape(1, WIDTH)

    pl.semaphore_wait(barrier, len(peers))

    kv_copies = [
        rcopy(k, kall.at[pl.ds(TOK, TOK)], s_kv.at[0], r_kv.at[0], far),
        rcopy(v, vall.at[pl.ds(TOK, TOK)], s_kv.at[1], r_kv.at[1], far),
    ]
    mine = pl.ds(pl.multiple_of(c * 40, 8), 40)
    wcore = rcopy(wf.at[mate], asm.at[mine], s_c.at[0], r_c.at[0], core)
    wcore.start()

    asm[mine, :] = wf[c]
    wcore.wait()
    wh[c, pair, y, zlo] = asm[...].astype(BF16)

    steps = (0, 7, 1, 6, 2, 5, 3, 4)

    def hop(e):
        there = lax.rem(pair + e // 4, 2) * 4 + lax.rem(zlo + e, 4)
        return there, lax.rem(there - z + NZ, NZ)

    def block(row, e):
        there = lax.rem(z + steps[e], NZ)
        return wh.at[c, there // 4, row, lax.rem(there, 4)]

    def zcopy(e):
        part = block(y, 0 if e <= 2 else e - 2)
        return rcopy(part, part, s_z.at[e], r_z.at[e], zdev(1 if e % 2 else 7))

    def ycopy(s, e):
        part = block(y, e)
        return rcopy(part, part, s_y.at[s, e], r_y.at[s, e], ydev(1 + 2 * s))

    def ypass(s, e):
        part = block(lax.rem(y + 3 - 2 * s, NY), e).at[:, pl.ds(s * HL, HL)]
        return rcopy(part, part, s_y.at[2 + s, e], r_y.at[2 + s, e], ydev(1 + 2 * s))

    def swap(e):
        there = lax.rem(z + steps[e], NZ)
        part = wh.at[c, there // 4, :, lax.rem(there, 4)]
        return rcopy(part, part, s_w.at[e], r_w.at[e], core)

    def yforward(e):
        for s in range(2):
            ycopy(s, e).wait_recv()
        for s in range(2):
            ypass(s, e).start()

    def hand(e):
        for s in range(2):
            ypass(s, e).wait_recv()
        swap(e).start()

    def serve(e):
        zcopy(e).wait_recv()
        if e + 2 < 8:
            zcopy(e + 2).start()
        for s in range(2):
            ycopy(s, e).start()
        yforward(e - 1)
        if e == 3:
            for cp in kv_copies:
                cp.start()
        if e >= 3:
            hand(e - 3)

    for e in (1, 2):
        zcopy(e).start()
    for s in range(2):
        ycopy(s, 0).start()

    scale2 = HEAD_DIM ** (-0.5) * LOG2E
    for cp in local:
        cp.wait()
    ktr[:, 0:TOK] = jnp.transpose(kall[0:TOK, :].astype(F32)).astype(BF16)
    vtr[:, 0:TOK] = jnp.transpose(vall[0:TOK, :].astype(F32)).astype(BF16)

    def softmax_part(h, rows):
        cols = pl.ds(pl.multiple_of(h * HEAD_DIM, HEAD_DIM), HEAD_DIM)
        s = mm(kall[rows, :], qv[:, cols], NT) * scale2 + bias[rows, :]
        top = jnp.max(s, axis=0, keepdims=True)
        e = jnp.exp2(s - top)
        total = jnp.sum(e, axis=0, keepdims=True)
        return top, total, mm(vtr[:, rows], e.astype(BF16), NN)

    def forward_own(h, carry):
        peak[h], mass[h], part_out[h] = softmax_part(h, pl.ds(0, TOK))
        return carry

    def forward_far(h, carry):
        top1, total1, out1 = peak[h], mass[h], part_out[h]
        top2, total2, out2 = softmax_part(h, pl.ds(TOK, TOK))
        top = jnp.maximum(top1, top2)
        fac1, fac2 = jnp.exp2(top1 - top), jnp.exp2(top2 - top)
        total = total1 * fac1 + total2 * fac2
        out = out1 * (fac1 / total) + out2 * (fac2 / total)
        lane = pl.ds(pl.multiple_of(lax.rem(h, 4) * HEAD_DIM, HEAD_DIM), HEAD_DIM)
        att[h // 4, :, lane] = jnp.transpose(out).astype(BF16)
        lse[h] = top + jnp.log2(total)
        return carry

    for e in range(1, 7):
        lax.fori_loop(e - 1, e, forward_own, 0)
        serve(e)
    lax.fori_loop(6, HEADS, forward_own, 0)
    serve(7)
    for cp in kv_copies:
        cp.wait()
    ktr[:, TOK:] = jnp.transpose(kall[TOK:, :].astype(F32)).astype(BF16)
    vtr[:, TOK:] = jnp.transpose(vall[TOK:, :].astype(F32)).astype(BF16)
    lax.fori_loop(0, 2, forward_far, 0)
    yforward(7)
    hand(5)
    lax.fori_loop(2, 6, forward_far, 0)
    hand(6)
    hand(7)
    lax.fori_loop(6, HEADS, forward_far, 0)

    def wrows(half, j):
        return wh[half, j // 2, pl.ds(lax.rem(j, 2) * 2, 2)].reshape(CW, HALF)

    def project_own(i, carry):
        j = lax.rem(i + 2 * pair, CHUNKS)
        acc[j] = mm(att[c], wrows(c, j), NT).reshape(NX, ROWS, CW)
        return carry

    def xcopy(kind, t, j):
        near = 1 + 2 * t
        if kind == 0:
            src, dst = xs.at[j, lax.rem(x + 2, NX), pl.ds(HR * t, HR)], xrel.at[t, j]
        elif kind == 1:
            rows = pl.ds(HR * (1 - t), HR)
            src, dst = xs.at[j, lax.rem(x + near, NX), rows], xin.at[t, j, rows]
        else:
            src, dst = xro.at[t, j], xin.at[t, j, pl.ds(HR * t, HR)]
        return rcopy(src, dst, s_x.at[kind, t, j], r_x.at[kind, t, j], xdev(near))

    def xstart(i):
        j = lax.rem(i + 2 * pair, CHUNKS)
        for kind in range(2):
            for t in range(2):
                xcopy(kind, t, j).start()

    def xsent(i):
        j = lax.rem(i + 2 * pair, CHUNKS)
        for kind in range(2):
            for t in range(2):
                xcopy(kind, t, j).wait_send()

    def project_rest(i, carry):
        j = lax.rem(i + 2 * pair, CHUNKS)
        p = acc[j] + mm(att[mate], wrows(mate, j), NT).reshape(NX, ROWS, CW)
        acc[j] = p
        xs[j] = p.astype(BF16)
        return carry

    def xforward(i, carry):
        j = lax.rem(i + 2 * pair, CHUNKS)
        for t in range(2):
            xcopy(0, t, j).wait_recv()
            mine_too = acc[j, lax.rem(x + 1 + 2 * t, NX), pl.ds(HR * t, HR)]
            xro[t, j] = (mine_too + xrel[t, j].astype(F32)).astype(BF16)
            xcopy(2, t, j).start()
        return carry

    lax.fori_loop(0, CHUNKS, project_own, 0)
    for e in range(8):
        swap(e).wait()
    project_rest(0, 0)
    xstart(0)
    lax.fori_loop(1, CHUNKS, project_rest, 0)

    def xstep(i, carry):
        xsent(i - 1)
        xstart(i)
        xforward(i - 1, 0)
        return carry

    lax.fori_loop(1, CHUNKS, xstep, 0)
    xsent(CHUNKS - 1)
    xforward(CHUNKS - 1, 0)
    for e in range(8):
        if e > 0:
            zcopy(e).wait_send()
        for s in range(2):
            ycopy(s, e).wait_send()
            ypass(s, e).wait_send()
    load_hidden.wait()

    def layer_copy(j):
        cols = pl.ds(pl.multiple_of(j * CW, 128), CW)
        return pltpu.make_async_copy(lv.at[:, cols], layer_o.at[:, cols], out_l.at[j])

    def layer(i, carry):
        square, along = carry
        j = lax.rem(i + 2 * pair, CHUNKS)
        for t in range(2):
            xcopy(1, t, j).wait_recv()
            xcopy(2, t, j).wait()
        cols = pl.ds(pl.multiple_of(j * CW, 128), CW)
        total = hv[:, cols].astype(F32) + acc[j, x]
        for t in range(2):
            total += xin[t, j].astype(F32)
        rounded = total.astype(BF16)
        lv[:, cols] = rounded
        layer_copy(j).start()
        value = rounded.astype(F32)
        square += jnp.sum(value * value, axis=1, keepdims=True)
        along += jnp.sum(value * factor[:, cols], axis=1, keepdims=True)
        return square, along

    zero = jnp.zeros((ROWS, 1), F32)
    square, along = lax.fori_loop(0, CHUNKS, layer, (zero, zero))
    inv = lax.rsqrt(square * (1.0 / WIDTH) + NORM_EPS)
    position = x * ROWS + lax.broadcasted_iota(jnp.int32, (ROWS, 1), 0)
    valid = jnp.where(position < len_own, 1.0, 0.0)
    root = jnp.sqrt(jnp.full((ROWS, 1), len_own, jnp.int32).astype(F32))
    weight = valid / root
    partial = jnp.sum(inv * along * weight, axis=0, keepdims=True)
    rw[pair, x] = jnp.broadcast_to(partial, (8, 128))
    own_rw = rw.at[pair, x]
    rw_far = rcopy(own_rw, own_rw, s_rw.at[0], r_rw.at[0], far)
    rw_far.start()
    both_rw = rw.at[:, x]
    rw_copies = [rcopy(both_rw, both_rw, s_rw.at[d], r_rw.at[d], xdev(d)) for d in (1, 2, 3)]

    gscale = inv * weight
    gcorr = inv * inv * inv * along * weight * (1.0 / WIDTH)

    def gcopy(kind, t, j):
        if kind == 0:
            part = gf.at[j, x]
        else:
            part = gf.at[j, lax.rem(x + 3 - 2 * t, NX), pl.ds(HR * t, HR)]
        return rcopy(part, part, s_g.at[kind, t, j], r_g.at[kind, t, j], xdev(1 + 2 * t))

    def rows_grad(i, carry):
        j = lax.rem(i + 2 * pair, CHUNKS)
        cols = pl.ds(pl.multiple_of(j * CW, 128), CW)
        value = lv[:, cols].astype(F32)
        gf[j, x] = (gscale * factor[:, cols] - value * gcorr).astype(BF16)
        for t in range(2):
            @pl.when(i < 1)
            def _():
                gcopy(0, t, j).start()
        return carry

    lax.fori_loop(0, CHUNKS, rows_grad, 0)

    def gforward(i):
        j = lax.rem(i + 2 * pair, CHUNKS)
        for t in range(2):
            gcopy(0, t, j).wait_send()
        if i + 1 < CHUNKS:
            for t in range(2):
                gcopy(0, t, lax.rem(j + 1, CHUNKS)).start()
        for t in range(2):
            gcopy(0, t, j).wait_recv()
        for t in range(2):
            gcopy(1, t, j).start()

    rw_far.wait()
    for cp in rw_copies:
        cp.start()
    gforward(0)
    gforward(1)
    for cp in rw_copies:
        cp.wait()
    reward0 = rw[0, 0] + rw[0, 1] + rw[0, 2] + rw[0, 3]
    reward1 = rw[1, 0] + rw[1, 1] + rw[1, 2] + rw[1, 3]
    sign = 2.0 * jnp.full((8, 128), labels[0], jnp.int32).astype(F32) - 1.0
    margin = sign * (reward0 - reward1)
    loss_o[...] = jnp.maximum(-margin, 0.0) + jnp.log1p(jnp.exp(-jnp.abs(margin)))
    first = -sign * jax.nn.sigmoid(-margin) * LOSS_SCALE
    side = jnp.where(pair == 0, 1.0, -1.0)
    slope = (first * side)[0:1, 0:1]

    def mcopy(j):
        return rcopy(mo.at[j], mi.at[j], s_m.at[j], r_m.at[j], core)

    gacc[...] = jnp.zeros_like(gacc)

    def products(i):
        j = lax.rem(i + 2 * pair, CHUNKS)
        for t in range(2):
            gcopy(1, t, j).wait()
        g = gf[j].reshape(TOK, CW)
        mo[j] = (mm(g, att[mate], TN) * slope).astype(BF16)
        mcopy(j).start()
        own[j] = mm(g, att[c], TN) * slope
        for half in range(2):
            gacc[half] += mm(g, wrows(half, j), NN)

    def ycopy2(kind, s, zh):
        near = 1 + 2 * s
        if kind == 0:
            src = red.at[zh, lax.rem(y + 2, NY), pl.ds(2 * s, 2), :, pl.ds(0, LA)]
            dst = yrel.at[s, zh]
        elif kind == 1:
            blocks = pl.ds(2 - 2 * s, 2)
            src = red.at[zh, lax.rem(y + near, NY), blocks, :, pl.ds(0, LA)]
            dst = yin.at[s, zh, blocks]
        else:
            src, dst = yro.at[s, zh], yin.at[s, zh, pl.ds(2 * s, 2)]
        return rcopy(src, dst, t_y.at[kind, s, zh], u_y.at[kind, s, zh], ydev(near))

    def zcopy3(d, yp):
        to = lax.rem(z + d, NZ)
        src = red.at[to // 4, pl.ds(2 * yp, 2), lax.rem(to, 4), :, pl.ds(LA, LB)]
        return rcopy(src, z2l.at[d - 1, yp], t_z2.at[d - 1, yp], u_z2.at[d - 1, yp], zdev(d))

    def merge(i):
        j = lax.rem(i + 2 * pair, CHUNKS)
        zh = j // 2
        yp = lax.rem(j, 2)
        mcopy(j).wait()
        both = own[j] + mi[j].astype(F32)
        red[zh, pl.ds(yp * 2, 2)] = both.astype(BF16).reshape(2, 4, BLK, HALF)

        @pl.when(lax.rem(y + 2, NY) // 2 == yp)
        def _():
            for s in range(2):
                ycopy2(0, s, zh).start()

        for s in range(2):
            @pl.when(lax.rem(y + 1 + 2 * s, NY) // 2 == yp)
            def _():
                ycopy2(1, s, zh).start()

        for d in (4, 3, 5, 2, 6, 1, 7):
            @pl.when(lax.rem(z + d, NZ) // 4 == zh)
            def _():
                zcopy3(d, yp).start()

    def yrelay(part):
        zh = lax.rem(pair + part, 2)
        for s in range(2):
            ycopy2(0, s, zh).wait_recv()
            mine_too = red[zh, lax.rem(y + 1 + 2 * s, NY), pl.ds(2 * s, 2), :, pl.ds(0, LA)].astype(F32)
            yro[s, zh] = (mine_too + yrel[s, zh].astype(F32)).astype(BF16)
            ycopy2(2, s, zh).start()

    products(0)
    gforward(2)
    products(1)
    merge(0)
    gforward(3)
    products(2)
    merge(1)
    products(3)
    merge(2)
    merge(3)

    gatt[...] = gacc[...].astype(BF16)
    dk[...] = jnp.zeros_like(dk)
    dv[...] = jnp.zeros_like(dv)
    slope_scaled = slope * HEAD_DIM ** (-0.5)

    def dq_copy(h):
        cols = pl.ds(pl.multiple_of(h * HEAD_DIM, HEAD_DIM), HEAD_DIM)
        return pltpu.make_async_copy(dqv.at[:, cols], dq_o.at[:, cols], out_q.at[h])

    def backward(h, carry):
        cols = pl.ds(pl.multiple_of(h * HEAD_DIM, HEAD_DIM), HEAD_DIM)
        lane = pl.ds(pl.multiple_of(lax.rem(h, 4) * HEAD_DIM, HEAD_DIM), HEAD_DIM)
        qh = qv[:, cols]
        gh = gatt[h // 4, :, lane]
        p = jnp.exp2(mm(kall[...], qh, NT) * scale2 + bias[...] - lse[h])
        dprob = mm(vall[...], gh, NT)
        delta = jnp.sum(p * dprob, axis=0, keepdims=True)
        ds = (p * (dprob - delta)).astype(BF16)
        dv[...] += mm(p.astype(BF16), gh, NN)
        dk[...] += mm(ds, qh, NN)
        dqv[:, cols] = (jnp.transpose(mm(ktr[...], ds, NN)) * slope_scaled).astype(BF16)
        dq_copy(h).start()
        return carry

    def zcopy2(d):
        to = lax.rem(z + d, NZ)
        src = zsend.at[to // 4, lax.rem(to, 4)]
        return rcopy(src, zl.at[d - 1], t_z.at[d - 1], u_z.at[d - 1], zdev(d))

    def ysum(part):
        zh = lax.rem(pair + part, 2)
        total = red[zh, y, :, :, pl.ds(0, LA)].astype(F32)
        for s in range(2):
            ycopy2(1, s, zh).wait_recv()
            ycopy2(2, s, zh).wait_recv()
            total += yin[s, zh].astype(F32)
        zsend[zh] = total.astype(BF16)
        for e in range(4 * part, 4 * part + 4):
            if e > 0:
                zcopy2(hop(e)[1]).start()

    lax.fori_loop(0, 2, backward, 0)
    yrelay(0)
    lax.fori_loop(2, 6, backward, 0)
    yrelay(1)
    lax.fori_loop(6, HEADS, backward, 0)

    dkv_out[0] = (dk[TOK:, :] * slope_scaled).astype(BF16)
    dkv_out[1] = (dv[TOK:, :] * slope).astype(BF16)
    back = [rcopy(dkv_out.at[i], dkv_in.at[i], s_kv.at[2 + i], r_kv.at[2 + i], far) for i in range(2)]
    for cp in back:
        cp.start()

    ysum(0)
    ysum(1)
    total = red[pair, :, zlo, :, pl.ds(LA, LB)].astype(F32).reshape(2, 2, BLK, LB)
    for d in range(1, 8):
        for yp in range(2):
            zcopy3(d, yp).wait()
        total += z2l[d - 1].astype(F32)
    y2send[...] = total.astype(BF16).reshape(NY, BLK, LB)
    yb2 = []
    for d in (2, 1, 3):
        src = y2send.at[lax.rem(y + d, NY)]
        yb2.append(rcopy(src, y2l.at[d - 1], t_y2.at[d - 1], u_y2.at[d - 1], ydev(d)))
        yb2[-1].start()
    for d in range(1, 8):
        zcopy2(d).wait()
    for kind in range(3):
        for s in range(2):
            for zh in range(2):
                ycopy2(kind, s, zh).wait_send()
    total = zsend[pair, zlo].astype(F32)
    for d in range(7):
        total += zl[d].astype(F32)
    gwc[:, 0:LA] = total
    for cp in yb2:
        cp.wait()
    total = y2send[y].astype(F32)
    for d in range(3):
        total += y2l[d].astype(F32)
    gwc[:, LA:] = total
    mate_rows = gwc.at[pl.ds(pl.multiple_of(mate * 40, 8), 40)]
    gswap = rcopy(mate_rows, gwr, s_c.at[3], r_c.at[3], core)
    gswap.start()
    gw_o[:, pl.ds(pl.multiple_of(c * HALF, HALF), HALF)] = gwc[mine, :]
    gswap.wait()
    gw_o[:, pl.ds(pl.multiple_of(mate * HALF, HALF), HALF)] = gwr[...]

    for j in range(CHUNKS):
        layer_copy(j).wait()
    for h in range(HEADS):
        dq_copy(h).wait()
    for cp in back:
        cp.wait()
    dk_o[...] = (dk[0:TOK, :] * slope_scaled + dkv_in[0].astype(F32)).astype(BF16)
    dv_o[...] = (dv[0:TOK, :] * slope + dkv_in[1].astype(F32)).astype(BF16)


def place(*refs):
    for source, result in zip(refs[:5], refs[6:]):
        result[...] = source[...]
    refs[11][0] = jnp.max(refs[5][...])


def per_device(hidden_in, queries, key_states, value_states, out_weight, norm_gain, reward_head, lengths, labels):
    smem = pl.BlockSpec(memory_space=pltpu.SMEM)
    vmem = pl.BlockSpec(memory_space=pltpu.VMEM)
    hbm = pl.BlockSpec(memory_space=pl.ANY)
    layer_rows, loss, grad_query, grad_keys, grad_values, grad_weight = pl.pallas_call(
        kernel,
        out_shape=(
            jax.ShapeDtypeStruct((ROWS, WIDTH), BF16),
            jax.ShapeDtypeStruct((8, 128), F32),
            jax.ShapeDtypeStruct((TOK, HEADS * HEAD_DIM), BF16),
            jax.ShapeDtypeStruct((TOK, HEAD_DIM), BF16),
            jax.ShapeDtypeStruct((TOK, HEAD_DIM), BF16),
            jax.ShapeDtypeStruct((40, 2 * HALF), F32),
        ),
        in_specs=[smem, smem] + [hbm] * 4 + [vmem] * 3,
        out_specs=(hbm, vmem, hbm, vmem, vmem, vmem),
        scratch_shapes=list(SCRATCH.values()),
        compiler_params=pltpu.CompilerParams(
            collective_id=0, has_side_effects=True, vmem_limit_bytes=60 * 2**20
        ),
        cost_estimate=pl.CostEstimate(flops=12 * 10**9, bytes_accessed=10 * 2**20, transcendentals=0),
    )(
        lengths,
        labels,
        hidden_in[0, 0],
        queries[0, 0],
        key_states[0, 0],
        value_states[0, 0],
        out_weight.T,
        norm_gain,
        reward_head,
    )
    results = (layer_rows, grad_query, grad_keys, grad_values, grad_weight)
    shapes = tuple(jax.ShapeDtypeStruct(r.shape, r.dtype) for r in results)
    layer_rows, grad_query, grad_keys, grad_values, grad_weight, loss = pl.pallas_call(
        place,
        out_shape=shapes + (jax.ShapeDtypeStruct((1,), F32),),
        in_specs=[vmem] * 6,
        out_specs=(vmem,) * 5 + (smem,),
        cost_estimate=pl.CostEstimate(flops=0, bytes_accessed=4 * 2**20, transcendentals=0),
    )(*results, loss)
    return (
        layer_rows[None, None],
        loss,
        grad_query[None, None],
        grad_keys[None, None],
        grad_values[None, None],
        grad_weight.T,
    )


def solution(mesh):
    in_specs = (
        P("dp", "pair", "tensor", None),
        P("dp", "pair", None, "tensor"),
        P("dp", "pair", None, "tensor"),
        P("dp", "pair", None, "tensor"),
        P("tensor", ("pair", "dp")),
        P(),
        P(),
        P("dp", None),
        P("dp"),
    )
    out_specs = (
        P("dp", "pair", "tensor", None),
        P("dp"),
        P("dp", "pair", None, "tensor"),
        P("dp", "pair", None, "tensor"),
        P("dp", "pair", None, "tensor"),
        P("tensor", ("pair", "dp")),
    )
    return jax.shard_map(
        per_device, mesh=mesh, in_specs=in_specs, out_specs=out_specs, check_vma=False
    )
```

```python
from types import SimpleNamespace

import jax
import jax.numpy as jnp
from jax import lax
from jax.experimental import pallas as pl
from jax.experimental.pallas import tpu as pltpu
from jax.sharding import PartitionSpec as P

HEAD_DIM = 128
LOSS_SCALE = 1024.0
NORM_EPS = 1e-06
LOG2E = 1.4426950408889634

TOK = 384
WIDTH = 2560
HEADS = 8
NX, NY, NZ = 4, 4, 8
ROWS = TOK // NX
CHUNKS = 4
CW = WIDTH // CHUNKS
BLK = 80
HALF = 512
HR = ROWS // 2
HL = HALF // 2
LA = 384
LB = HALF - LA

MESH = pl.DeviceIdType.MESH
F32 = jnp.float32
BF16 = jnp.bfloat16

NT = (((1,), (1,)), ((), ()))
TN = (((0,), (0,)), ((), ()))
NN = (((1,), (0,)), ((), ()))


def mm(a, b, dims):
    return lax.dot_general(a, b, dims, preferred_element_type=F32)


def device(x, y, z, c):
    return (z // 4, x, y * 8 + lax.rem(z, 4) * 2 + c)


def rcopy(src, dst, send, recv, dev):
    return pltpu.make_async_remote_copy(
        src_ref=src, dst_ref=dst, send_sem=send, recv_sem=recv, device_id=dev, device_id_type=MESH
    )


DMA = pltpu.SemaphoreType.DMA
ARGS = (
    "lens",
    "labels",
    "hidden",
    "q",
    "k",
    "v",
    "wt",
    "gain",
    "head",
    "layer_o",
    "loss_o",
    "dq_o",
    "dk_o",
    "dv_o",
    "gw_o",
)
SCRATCH = dict(
    wh=pltpu.VMEM((2, 2, NY, 4, BLK, HALF), BF16),
    wf=pltpu.VMEM((2, 40, HALF), F32),
    qv=pltpu.VMEM((TOK, HEADS * HEAD_DIM), BF16),
    hv=pltpu.VMEM((ROWS, WIDTH), BF16),
    lv=pltpu.VMEM((ROWS, WIDTH), BF16),
    dqv=pltpu.VMEM((TOK, HEADS * HEAD_DIM), BF16),
    asm=pltpu.VMEM((BLK, HALF), F32),
    kall=pltpu.VMEM((2 * TOK, HEAD_DIM), BF16),
    vall=pltpu.VMEM((2 * TOK, HEAD_DIM), BF16),
    ktr=pltpu.VMEM((HEAD_DIM, 2 * TOK), BF16),
    vtr=pltpu.VMEM((HEAD_DIM, 2 * TOK), BF16),
    bias=pltpu.VMEM((2 * TOK, TOK), F32),
    peak=pltpu.VMEM((HEADS, 1, TOK), F32),
    mass=pltpu.VMEM((HEADS, 1, TOK), F32),
    part_out=pltpu.VMEM((HEADS, HEAD_DIM, TOK), F32),
    probs=pltpu.VMEM((HEADS, 2 * TOK, TOK), BF16),
    dscores=pltpu.VMEM((HEADS, 2 * TOK, TOK), BF16),
    lse=pltpu.VMEM((HEADS, 1, TOK), F32),
    att=pltpu.VMEM((2, TOK, HALF), BF16),
    acc=pltpu.VMEM((CHUNKS, NX, ROWS, CW), F32),
    xs=pltpu.VMEM((CHUNKS, NX, ROWS, CW), BF16),
    xin=pltpu.VMEM((2, CHUNKS, ROWS, CW), BF16),
    xrel=pltpu.VMEM((2, CHUNKS, HR, CW), BF16),
    xro=pltpu.VMEM((2, CHUNKS, HR, CW), BF16),
    gf=pltpu.VMEM((CHUNKS, NX, ROWS, CW), BF16),
    rw=pltpu.VMEM((2, NX, 8, 128), F32),
    own=pltpu.VMEM((CHUNKS, CW, HALF), F32),
    mo=pltpu.VMEM((CHUNKS, CW, HALF), BF16),
    mi=pltpu.VMEM((CHUNKS, CW, HALF), BF16),
    red=pltpu.VMEM((2, NY, 4, BLK, HALF), BF16),
    yin=pltpu.VMEM((2, 2, 4, BLK, LA), BF16),
    yrel=pltpu.VMEM((2, 2, 2, BLK, LA), BF16),
    yro=pltpu.VMEM((2, 2, 2, BLK, LA), BF16),
    zsend=pltpu.VMEM((2, 4, BLK, LA), BF16),
    zl=pltpu.VMEM((7, BLK, LA), BF16),
    z2l=pltpu.VMEM((2, 2, 2, 2, BLK, LB), BF16),
    z2third=pltpu.VMEM((2, 2, 2, BLK, LB), BF16),
    z2fourth=pltpu.VMEM((2, 2, 1, BLK, LB), BF16),
    z2out=pltpu.VMEM((2, 2, 2, BLK, LB), BF16),
    y2send=pltpu.VMEM((NY, BLK, LB), BF16),
    y2l=pltpu.VMEM((3, BLK, LB), BF16),
    factor=pltpu.VMEM((1, WIDTH), F32),
    gwc=pltpu.VMEM((BLK, HALF), F32),
    gwr=pltpu.VMEM((40, HALF), F32),
    gacc=pltpu.VMEM((2, TOK, HALF), F32),
    gatt=pltpu.VMEM((2, TOK, HALF), BF16),
    dk=pltpu.VMEM((2 * TOK, HEAD_DIM), F32),
    dv=pltpu.VMEM((2 * TOK, HEAD_DIM), F32),
    dkv_out=pltpu.VMEM((2, TOK, HEAD_DIM), BF16),
    dkv_in=pltpu.VMEM((2, TOK, HEAD_DIM), BF16),
    s_kv=DMA((4,)),
    r_kv=DMA((4,)),
    s_c=DMA((4,)),
    r_c=DMA((4,)),
    s_z=DMA((8,)),
    r_z=DMA((8,)),
    s_w=DMA((8,)),
    r_w=DMA((8,)),
    s_y=DMA((4, 8)),
    r_y=DMA((4, 8)),
    s_x=DMA((3, 2, CHUNKS)),
    r_x=DMA((3, 2, CHUNKS)),
    s_g=DMA((2, 2, CHUNKS)),
    r_g=DMA((2, 2, CHUNKS)),
    s_rw=DMA((4,)),
    r_rw=DMA((4,)),
    s_m=DMA((CHUNKS,)),
    r_m=DMA((CHUNKS,)),
    t_z=DMA((7,)),
    u_z=DMA((7,)),
    t_y=DMA((3, 2, 2)),
    u_y=DMA((3, 2, 2)),
    t_z2=DMA((4, 2, 2)),
    u_z2=DMA((4, 2, 2)),
    loc=DMA((8,)),
    out_l=DMA((CHUNKS,)),
    out_q=DMA((HEADS,)),
    t_y2=DMA((3,)),
    u_y2=DMA((3,)),
)


def kernel(*refs):
    names = SimpleNamespace(**dict(zip(ARGS + tuple(SCRATCH), refs)))
    run(names)


def run(n):
    lens = n.lens
    labels = n.labels
    hidden = n.hidden
    q = n.q
    k = n.k
    v = n.v
    wt = n.wt
    gain = n.gain
    head = n.head
    layer_o = n.layer_o
    loss_o = n.loss_o
    dq_o = n.dq_o
    dk_o = n.dk_o
    dv_o = n.dv_o
    gw_o = n.gw_o
    wh = n.wh
    wf = n.wf
    qv = n.qv
    hv = n.hv
    lv = n.lv
    dqv = n.dqv
    asm = n.asm
    kall = n.kall
    vall = n.vall
    ktr = n.ktr
    vtr = n.vtr
    bias = n.bias
    peak = n.peak
    mass = n.mass
    part_out = n.part_out
    probs = n.probs
    dscores = n.dscores
    lse = n.lse
    att = n.att
    acc = n.acc
    xs = n.xs
    xin = n.xin
    xrel = n.xrel
    xro = n.xro
    gf = n.gf
    rw = n.rw
    own = n.own
    mo = n.mo
    mi = n.mi
    red = n.red
    yin = n.yin
    yrel = n.yrel
    yro = n.yro
    zsend = n.zsend
    zl = n.zl
    z2l = n.z2l
    z2third = n.z2third
    z2fourth = n.z2fourth
    z2out = n.z2out
    y2send = n.y2send
    y2l = n.y2l
    factor = n.factor
    gwc = n.gwc
    gwr = n.gwr
    gacc = n.gacc
    gatt = n.gatt
    dk = n.dk
    dv = n.dv
    dkv_out = n.dkv_out
    dkv_in = n.dkv_in
    s_kv = n.s_kv
    r_kv = n.r_kv
    s_c = n.s_c
    r_c = n.r_c
    s_z = n.s_z
    r_z = n.r_z
    s_w = n.s_w
    r_w = n.r_w
    s_y = n.s_y
    r_y = n.r_y
    s_x = n.s_x
    r_x = n.r_x
    s_g = n.s_g
    r_g = n.r_g
    s_rw = n.s_rw
    r_rw = n.r_rw
    s_m = n.s_m
    r_m = n.r_m
    t_z = n.t_z
    u_z = n.u_z
    t_y = n.t_y
    u_y = n.u_y
    t_z2 = n.t_z2
    u_z2 = n.u_z2
    loc = n.loc
    out_l = n.out_l
    out_q = n.out_q
    t_y2 = n.t_y2
    u_y2 = n.u_y2

    pair = lax.axis_index("pair")
    x = lax.axis_index("tensor")
    dp = lax.axis_index("dp")
    y = dp // 8
    zlo = lax.rem(dp // 2, 4)
    z = pair * 4 + zlo
    c = lax.rem(dp, 2)
    mate = 1 - c

    def xdev(d):
        return device(lax.rem(x + d, NX), y, z, c)

    def ydev(d):
        return device(x, lax.rem(y + d, NY), z, c)

    def zdev(d):
        return device(x, y, lax.rem(z + d, NZ), c)

    core = device(x, y, z, mate)
    far = zdev(4)

    local = [
        pltpu.make_async_copy(k, kall.at[pl.ds(0, TOK)], loc.at[0]),
        pltpu.make_async_copy(v, vall.at[pl.ds(0, TOK)], loc.at[1]),
        pltpu.make_async_copy(q, qv, loc.at[2]),
    ]
    load_hidden = pltpu.make_async_copy(hidden, hv, loc.at[3])
    for cp in local + [load_hidden]:
        cp.start()

    barrier = pltpu.get_barrier_semaphore()
    peers = [core]
    peers += [xdev(d) for d in (1, 2, 3)]
    peers += [ydev(d) for d in (1, 2, 3)]
    peers += [zdev(d) for d in range(1, NZ)]
    for peer in peers:
        pl.semaphore_signal(barrier, inc=1, device_id=peer, device_id_type=MESH)

    len_own = jnp.where(pair == 0, lens[0, 0], lens[0, 1])
    len_par = jnp.where(pair == 0, lens[0, 1], lens[0, 0])
    key_id = lax.broadcasted_iota(jnp.int32, (TOK, TOK), 0)
    tok_id = lax.broadcasted_iota(jnp.int32, (TOK, TOK), 1)
    bias[0:TOK, :] = jnp.where((key_id <= tok_id) & (key_id < len_own), 0.0, -1e30)
    bias[TOK:, :] = jnp.where(key_id < len_par, 0.0, -1e30)

    for half in range(2):
        wf[half] = wt[:, pl.ds(half * HALF, HALF)].astype(F32)

    factor[...] = (gain[...] * head[...]).reshape(1, WIDTH)

    pl.semaphore_wait(barrier, len(peers))

    kv_copies = [
        rcopy(k, kall.at[pl.ds(TOK, TOK)], s_kv.at[0], r_kv.at[0], far),
        rcopy(v, vall.at[pl.ds(TOK, TOK)], s_kv.at[1], r_kv.at[1], far),
    ]
    mine = pl.ds(pl.multiple_of(c * 40, 8), 40)
    wcore = rcopy(wf.at[mate], asm.at[mine], s_c.at[0], r_c.at[0], core)
    wcore.start()

    asm[mine, :] = wf[c]
    wcore.wait()
    wh[c, pair, y, zlo] = asm[...].astype(BF16)

    steps = (0, 7, 1, 6, 2, 5, 3, 4)

    def hop(e):
        there = lax.rem(pair + e // 4, 2) * 4 + lax.rem(zlo + e, 4)
        return there, lax.rem(there - z + NZ, NZ)

    def block(row, e):
        there = lax.rem(z + steps[e], NZ)
        return wh.at[c, there // 4, row, lax.rem(there, 4)]

    def zcopy(e):
        part = block(y, 0 if e <= 2 else e - 2)
        return rcopy(part, part, s_z.at[e], r_z.at[e], zdev(1 if e % 2 else 7))

    def ycopy(s, e):
        part = block(y, e)
        return rcopy(part, part, s_y.at[s, e], r_y.at[s, e], ydev(1 + 2 * s))

    def ypass(s, e):
        part = block(lax.rem(y + 3 - 2 * s, NY), e).at[:, pl.ds(s * HL, HL)]
        return rcopy(part, part, s_y.at[2 + s, e], r_y.at[2 + s, e], ydev(1 + 2 * s))

    def swap(e):
        there = lax.rem(z + steps[e], NZ)
        part = wh.at[c, there // 4, :, lax.rem(there, 4)]
        return rcopy(part, part, s_w.at[e], r_w.at[e], core)

    def yforward(e):
        for s in range(2):
            ycopy(s, e).wait_recv()
        for s in range(2):
            ypass(s, e).start()

    def hand(e):
        for s in range(2):
            ypass(s, e).wait_recv()
        swap(e).start()

    def serve(e):
        zcopy(e).wait_recv()
        if e + 2 < 8:
            zcopy(e + 2).start()
        for s in range(2):
            ycopy(s, e).start()
        yforward(e - 1)
        if e == 3:
            for cp in kv_copies:
                cp.start()
        if e >= 3:
            hand(e - 3)

    for e in (1, 2):
        zcopy(e).start()
    for s in range(2):
        ycopy(s, 0).start()

    scale2 = HEAD_DIM ** (-0.5) * LOG2E
    for cp in local:
        cp.wait()
    ktr[:, 0:TOK] = jnp.transpose(kall[0:TOK, :].astype(F32)).astype(BF16)
    vtr[:, 0:TOK] = jnp.transpose(vall[0:TOK, :].astype(F32)).astype(BF16)

    def softmax_part(h, rows):
        cols = pl.ds(pl.multiple_of(h * HEAD_DIM, HEAD_DIM), HEAD_DIM)
        s = mm(kall[rows, :], qv[:, cols], NT) * scale2 + bias[rows, :]
        top = jnp.max(s, axis=0, keepdims=True)
        e = jnp.exp2(s - top)
        total = jnp.sum(e, axis=0, keepdims=True)
        return top, total, mm(vtr[:, rows], e.astype(BF16), NN)

    def forward_own(h, carry):
        peak[h], mass[h], part_out[h] = softmax_part(h, pl.ds(0, TOK))
        return carry

    def forward_far(h, carry):
        top1, total1, out1 = peak[h], mass[h], part_out[h]
        top2, total2, out2 = softmax_part(h, pl.ds(TOK, TOK))
        top = jnp.maximum(top1, top2)
        fac1, fac2 = jnp.exp2(top1 - top), jnp.exp2(top2 - top)
        total = total1 * fac1 + total2 * fac2
        out = out1 * (fac1 / total) + out2 * (fac2 / total)
        lane = pl.ds(pl.multiple_of(lax.rem(h, 4) * HEAD_DIM, HEAD_DIM), HEAD_DIM)
        att[h // 4, :, lane] = jnp.transpose(out).astype(BF16)
        lse[h] = top + jnp.log2(total)
        return carry

    for e in range(1, 7):
        lax.fori_loop(e - 1, e, forward_own, 0)
        serve(e)
    lax.fori_loop(6, HEADS, forward_own, 0)
    serve(7)
    for cp in kv_copies:
        cp.wait()
    ktr[:, TOK:] = jnp.transpose(kall[TOK:, :].astype(F32)).astype(BF16)
    vtr[:, TOK:] = jnp.transpose(vall[TOK:, :].astype(F32)).astype(BF16)
    lax.fori_loop(0, 2, forward_far, 0)
    yforward(7)
    hand(5)
    lax.fori_loop(2, HEADS, forward_far, 0)
    hand(6)

    def wrows(half, j):
        return wh[half, j // 2, pl.ds(lax.rem(j, 2) * 2, 2)].reshape(CW, HALF)

    def project_own(i, carry):
        j = lax.rem(i + 2 * pair, CHUNKS)
        acc[j] = mm(att[c], wrows(c, j), NT).reshape(NX, ROWS, CW)
        return carry

    def xcopy(kind, t, j):
        near = 1 + 2 * t
        if kind == 0:
            src, dst = xs.at[j, lax.rem(x + 2, NX), pl.ds(HR * t, HR)], xrel.at[t, j]
        elif kind == 1:
            rows = pl.ds(HR * (1 - t), HR)
            src, dst = xs.at[j, lax.rem(x + near, NX), rows], xin.at[t, j, rows]
        else:
            src, dst = xro.at[t, j], xin.at[t, j, pl.ds(HR * t, HR)]
        return rcopy(src, dst, s_x.at[kind, t, j], r_x.at[kind, t, j], xdev(near))

    def xstart(i):
        j = lax.rem(i + 2 * pair, CHUNKS)
        for kind in range(2):
            for t in range(2):
                xcopy(kind, t, j).start()

    def xsent(i):
        j = lax.rem(i + 2 * pair, CHUNKS)
        for kind in range(2):
            for t in range(2):
                xcopy(kind, t, j).wait_send()

    def project_rest(i, carry):
        j = lax.rem(i + 2 * pair, CHUNKS)
        p = acc[j] + mm(att[mate], wrows(mate, j), NT).reshape(NX, ROWS, CW)
        acc[j] = p
        xs[j] = p.astype(BF16)
        return carry

    def xforward(i, carry):
        j = lax.rem(i + 2 * pair, CHUNKS)
        for t in range(2):
            xcopy(0, t, j).wait_recv()
            mine_too = acc[j, lax.rem(x + 1 + 2 * t, NX), pl.ds(HR * t, HR)]
            xro[t, j] = (mine_too + xrel[t, j].astype(F32)).astype(BF16)
            xcopy(2, t, j).start()
        return carry

    def probability(h, carry):
        cols = pl.ds(pl.multiple_of(h * HEAD_DIM, HEAD_DIM), HEAD_DIM)
        s = mm(kall[...], qv[:, cols], NT) * scale2 + bias[...]
        probs[h] = jnp.exp2(s - lse[h]).astype(BF16)
        return carry

    lax.fori_loop(0, 2, project_own, 0)
    for e in range(7):
        swap(e).wait()
    project_rest(0, 0)
    xstart(0)
    project_rest(1, 0)
    hand(7)
    lax.fori_loop(2, CHUNKS, project_own, 0)
    swap(7).wait()
    lax.fori_loop(2, CHUNKS, project_rest, 0)

    def xstep(i, carry):
        xsent(i - 1)
        xstart(i)
        xforward(i - 1, 0)
        lax.fori_loop(2 * i - 2, 2 * i, probability, 0)
        return carry

    lax.fori_loop(1, CHUNKS, xstep, 0)
    xsent(CHUNKS - 1)
    xforward(CHUNKS - 1, 0)
    lax.fori_loop(6, HEADS, probability, 0)
    for e in range(8):
        if e > 0:
            zcopy(e).wait_send()
        for s in range(2):
            ycopy(s, e).wait_send()
            ypass(s, e).wait_send()
    load_hidden.wait()

    def layer_copy(j):
        cols = pl.ds(pl.multiple_of(j * CW, 128), CW)
        return pltpu.make_async_copy(lv.at[:, cols], layer_o.at[:, cols], out_l.at[j])

    def layer(i, carry):
        square, along = carry
        j = lax.rem(i + 2 * pair, CHUNKS)
        for t in range(2):
            xcopy(1, t, j).wait_recv()
            xcopy(2, t, j).wait()
        cols = pl.ds(pl.multiple_of(j * CW, 128), CW)
        total = hv[:, cols].astype(F32) + acc[j, x]
        for t in range(2):
            total += xin[t, j].astype(F32)
        rounded = total.astype(BF16)
        lv[:, cols] = rounded
        layer_copy(j).start()
        value = rounded.astype(F32)
        square += jnp.sum(value * value, axis=1, keepdims=True)
        along += jnp.sum(value * factor[:, cols], axis=1, keepdims=True)
        return square, along

    zero = jnp.zeros((ROWS, 1), F32)
    square, along = lax.fori_loop(0, CHUNKS, layer, (zero, zero))
    inv = lax.rsqrt(square * (1.0 / WIDTH) + NORM_EPS)
    position = x * ROWS + lax.broadcasted_iota(jnp.int32, (ROWS, 1), 0)
    valid = jnp.where(position < len_own, 1.0, 0.0)
    root = jnp.sqrt(jnp.full((ROWS, 1), len_own, jnp.int32).astype(F32))
    weight = valid / root
    partial = jnp.sum(inv * along * weight, axis=0, keepdims=True)
    rw[pair, x] = jnp.broadcast_to(partial, (8, 128))
    own_rw = rw.at[pair, x]
    rw_far = rcopy(own_rw, own_rw, s_rw.at[0], r_rw.at[0], far)
    rw_far.start()
    both_rw = rw.at[:, x]
    rw_copies = [rcopy(both_rw, both_rw, s_rw.at[d], r_rw.at[d], xdev(d)) for d in (1, 2, 3)]

    gscale = inv * weight
    gcorr = inv * inv * inv * along * weight * (1.0 / WIDTH)

    def gcopy(kind, t, j):
        if kind == 0:
            part = gf.at[j, x]
        else:
            part = gf.at[j, lax.rem(x + 3 - 2 * t, NX), pl.ds(HR * t, HR)]
        return rcopy(part, part, s_g.at[kind, t, j], r_g.at[kind, t, j], xdev(1 + 2 * t))

    def rows_grad(i, carry):
        j = i
        cols = pl.ds(pl.multiple_of(j * CW, 128), CW)
        value = lv[:, cols].astype(F32)
        gf[j, x] = (gscale * factor[:, cols] - value * gcorr).astype(BF16)
        for t in range(2):
            @pl.when(i < 1)
            def _():
                gcopy(0, t, j).start()
        return carry

    lax.fori_loop(0, CHUNKS, rows_grad, 0)

    def gforward(i):
        j = i
        for t in range(2):
            gcopy(0, t, j).wait_send()
        if i + 1 < CHUNKS:
            for t in range(2):
                gcopy(0, t, lax.rem(j + 1, CHUNKS)).start()
        for t in range(2):
            gcopy(0, t, j).wait_recv()
        for t in range(2):
            gcopy(1, t, j).start()

    rw_far.wait()
    for cp in rw_copies:
        cp.start()
    gforward(0)
    gforward(1)
    for cp in rw_copies:
        cp.wait()
    reward0 = rw[0, 0] + rw[0, 1] + rw[0, 2] + rw[0, 3]
    reward1 = rw[1, 0] + rw[1, 1] + rw[1, 2] + rw[1, 3]
    sign = 2.0 * jnp.full((8, 128), labels[0], jnp.int32).astype(F32) - 1.0
    margin = sign * (reward0 - reward1)
    loss_o[...] = jnp.maximum(-margin, 0.0) + jnp.log1p(jnp.exp(-jnp.abs(margin)))
    first = -sign * jax.nn.sigmoid(-margin) * LOSS_SCALE
    side = jnp.where(pair == 0, 1.0, -1.0)
    slope = (first * side)[0:1, 0:1]

    def mcopy(j):
        return rcopy(mo.at[j], mi.at[j], s_m.at[j], r_m.at[j], core)

    gacc[...] = jnp.zeros_like(gacc)

    def products(i):
        j = i
        for t in range(2):
            gcopy(1, t, j).wait()
        g = gf[j].reshape(TOK, CW)
        mo[j] = (mm(g, att[mate], TN) * slope).astype(BF16)
        mcopy(j).start()
        own[j] = mm(g, att[c], TN) * slope
        for half in range(2):
            gacc[half] += mm(g, wrows(half, j), NN)

    def ycopy2(kind, s, zh):
        near = 1 + 2 * s
        if kind == 0:
            src = red.at[zh, lax.rem(y + 2, NY), pl.ds(2 * s, 2), :, pl.ds(0, LA)]
            dst = yrel.at[s, zh]
        elif kind == 1:
            blocks = pl.ds(2 - 2 * s, 2)
            src = red.at[zh, lax.rem(y + near, NY), blocks, :, pl.ds(0, LA)]
            dst = yin.at[s, zh, blocks]
        else:
            src, dst = yro.at[s, zh], yin.at[s, zh, pl.ds(2 * s, 2)]
        return rcopy(src, dst, t_y.at[kind, s, zh], u_y.at[kind, s, zh], ydev(near))

    def zblock(d, yp):
        to = lax.rem(z + d, NZ)
        return to // 4, pl.ds(2 * yp, 2), lax.rem(to, 4), slice(None), pl.ds(LA, LB)

    def zcopy3(kind, s, yp):
        near, over = (1, NZ - 1)[s], (2, NZ - 2)[s]
        sems = t_z2.at[kind, s, yp], u_z2.at[kind, s, yp]
        if kind == 0:
            return rcopy(red.at[zblock(near, yp)], z2l.at[s, 0, yp], *sems, zdev(near))
        if kind == 1:
            return rcopy(red.at[zblock((3, 5)[s], yp)], z2third.at[s, yp], *sems, zdev(near))
        if kind == 2:
            to = lax.rem(z + 4, NZ)
            src = red.at[to // 4, pl.ds(2 * yp + s, 1), lax.rem(to, 4), :, pl.ds(LA, LB)]
            return rcopy(src, z2fourth.at[s, yp], *sems, zdev(over))
        return rcopy(z2out.at[s, yp], z2l.at[s, 1, yp], *sems, zdev(over))

    def zrelay(i):
        zh, yp = i // 2, i % 2
        for s in range(2):
            over = (2, NZ - 2)[s]

            @pl.when(lax.rem(z + over, NZ) // 4 == zh)
            def _():
                zcopy3(1, s, yp).wait_recv()
                zcopy3(2, s, yp).wait_recv()
                both = red[zblock(over, yp)].astype(F32) + z2third[s, yp].astype(F32)
                z2out[s, yp, 1 - s] = both[1 - s].astype(BF16)
                z2out[s, yp, s] = (both[s] + z2fourth[s, yp, 0].astype(F32)).astype(BF16)
                zcopy3(3, s, yp).start()

    def merge(i):
        j = i
        zh, yp = j // 2, j % 2
        mcopy(j).wait()
        both = own[j] + mi[j].astype(F32)
        red[zh, pl.ds(yp * 2, 2)] = both.astype(BF16).reshape(2, 4, BLK, HALF)

        @pl.when(lax.rem(y + 2, NY) // 2 == yp)
        def _():
            for s in range(2):
                ycopy2(0, s, zh).start()

        for s in range(2):
            @pl.when(lax.rem(y + 1 + 2 * s, NY) // 2 == yp)
            def _():
                ycopy2(1, s, zh).start()

        for kind, spans in ((2, (4, 4)), (1, (3, 5)), (0, (1, 7))):
            for s in range(2):
                @pl.when(lax.rem(z + spans[s], NZ) // 4 == zh)
                def _():
                    zcopy3(kind, s, yp).start()

    def yrelay(zh):
        for s in range(2):
            ycopy2(0, s, zh).wait_recv()
            mine_too = red[zh, lax.rem(y + 1 + 2 * s, NY), pl.ds(2 * s, 2), :, pl.ds(0, LA)].astype(F32)
            yro[s, zh] = (mine_too + yrel[s, zh].astype(F32)).astype(BF16)
            ycopy2(2, s, zh).start()

    products(0)
    gforward(2)
    products(1)
    merge(0)
    gforward(3)
    products(2)
    merge(1)
    zrelay(0)
    products(3)
    merge(2)
    zrelay(1)
    merge(3)

    gatt[...] = gacc[...].astype(BF16)
    dk[...] = jnp.zeros_like(dk)
    dv[...] = jnp.zeros_like(dv)
    slope_scaled = slope * HEAD_DIM ** (-0.5)

    def dq_copy(h):
        cols = pl.ds(pl.multiple_of(h * HEAD_DIM, HEAD_DIM), HEAD_DIM)
        return pltpu.make_async_copy(dqv.at[:, cols], dq_o.at[:, cols], out_q.at[h])

    def backward(h, carry):
        cols = pl.ds(pl.multiple_of(h * HEAD_DIM, HEAD_DIM), HEAD_DIM)
        lane = pl.ds(pl.multiple_of(lax.rem(h, 4) * HEAD_DIM, HEAD_DIM), HEAD_DIM)
        gh = gatt[h // 4, :, lane]
        p = probs[h].astype(F32)
        dprob = mm(vall[...], gh, NT)
        delta = jnp.sum(p * dprob, axis=0, keepdims=True)
        dscores[h] = (p * (dprob - delta)).astype(BF16)
        dv[...] += mm(probs[h], gh, NN)
        dk[TOK:, :] += mm(dscores[h, TOK:, :], qv[:, cols], NN)
        return carry

    def backward_rest(h, carry):
        cols = pl.ds(pl.multiple_of(h * HEAD_DIM, HEAD_DIM), HEAD_DIM)
        dk[0:TOK, :] += mm(dscores[h, 0:TOK, :], qv[:, cols], NN)
        dqv[:, cols] = (jnp.transpose(mm(ktr[...], dscores[h], NN)) * slope_scaled).astype(BF16)
        dq_copy(h).start()
        return carry

    def zcopy2(d):
        to = lax.rem(z + d, NZ)
        src = zsend.at[to // 4, lax.rem(to, 4)]
        return rcopy(src, zl.at[d - 1], t_z.at[d - 1], u_z.at[d - 1], zdev(d))

    def ysum(zh):
        total = red[zh, y, :, :, pl.ds(0, LA)].astype(F32)
        for s in range(2):
            ycopy2(1, s, zh).wait_recv()
            ycopy2(2, s, zh).wait_recv()
            total += yin[s, zh].astype(F32)
        zsend[zh] = total.astype(BF16)

        @pl.when(pair != zh)
        def _():
            zcopy2(4).start()

        for e in (1, 2, 3):
            there = zh * 4 + lax.rem(zlo + e, 4)
            zcopy2(lax.rem(there - z + NZ, NZ)).start()

    lax.fori_loop(0, 3, backward, 0)
    zrelay(2)
    yrelay(0)
    lax.fori_loop(3, 5, backward, 0)
    zrelay(3)
    lax.fori_loop(5, HEADS, backward, 0)

    dkv_out[0] = (dk[TOK:, :] * slope_scaled).astype(BF16)
    dkv_out[1] = (dv[TOK:, :] * slope).astype(BF16)
    back = [rcopy(dkv_out.at[i], dkv_in.at[i], s_kv.at[2 + i], r_kv.at[2 + i], far) for i in range(2)]
    for cp in back:
        cp.start()

    yrelay(1)
    ysum(0)
    lax.fori_loop(0, HEADS, backward_rest, 0)
    ysum(1)
    total = red[pair, :, zlo, :, pl.ds(LA, LB)].astype(F32).reshape(2, 2, BLK, LB)
    for s in range(2):
        for kind in range(4):
            for yp in range(2):
                zcopy3(kind, s, yp).wait_send()
                if kind % 3 == 0:
                    zcopy3(kind, s, yp).wait_recv()
        for kind in range(2):
            total += z2l[s, kind].astype(F32)
    y2send[...] = total.astype(BF16).reshape(NY, BLK, LB)
    yb2 = []
    for d in (2, 1, 3):
        src = y2send.at[lax.rem(y + d, NY)]
        yb2.append(rcopy(src, y2l.at[d - 1], t_y2.at[d - 1], u_y2.at[d - 1], ydev(d)))
        yb2[-1].start()
    for d in range(1, 8):
        zcopy2(d).wait()
    for kind in range(3):
        for s in range(2):
            for zh in range(2):
                ycopy2(kind, s, zh).wait_send()
    total = zsend[pair, zlo].astype(F32)
    for d in range(7):
        total += zl[d].astype(F32)
    gwc[:, 0:LA] = total
    for cp in yb2:
        cp.wait()
    total = y2send[y].astype(F32)
    for d in range(3):
        total += y2l[d].astype(F32)
    gwc[:, LA:] = total
    mate_rows = gwc.at[pl.ds(pl.multiple_of(mate * 40, 8), 40)]
    gswap = rcopy(mate_rows, gwr, s_c.at[3], r_c.at[3], core)
    gswap.start()
    gw_o[:, pl.ds(pl.multiple_of(c * HALF, HALF), HALF)] = gwc[mine, :]
    gswap.wait()
    gw_o[:, pl.ds(pl.multiple_of(mate * HALF, HALF), HALF)] = gwr[...]

    for j in range(CHUNKS):
        layer_copy(j).wait()
    for h in range(HEADS):
        dq_copy(h).wait()
    for cp in back:
        cp.wait()
    dk_o[...] = (dk[0:TOK, :] * slope_scaled + dkv_in[0].astype(F32)).astype(BF16)
    dv_o[...] = (dv[0:TOK, :] * slope + dkv_in[1].astype(F32)).astype(BF16)


def place(*refs):
    for source, result in zip(refs[:5], refs[6:]):
        result[...] = source[...]
    refs[11][0] = jnp.max(refs[5][...])


def per_device(hidden_in, queries, key_states, value_states, out_weight, norm_gain, reward_head, lengths, labels):
    smem = pl.BlockSpec(memory_space=pltpu.SMEM)
    vmem = pl.BlockSpec(memory_space=pltpu.VMEM)
    hbm = pl.BlockSpec(memory_space=pl.ANY)
    layer_rows, loss, grad_query, grad_keys, grad_values, grad_weight = pl.pallas_call(
        kernel,
        out_shape=(
            jax.ShapeDtypeStruct((ROWS, WIDTH), BF16),
            jax.ShapeDtypeStruct((8, 128), F32),
            jax.ShapeDtypeStruct((TOK, HEADS * HEAD_DIM), BF16),
            jax.ShapeDtypeStruct((TOK, HEAD_DIM), BF16),
            jax.ShapeDtypeStruct((TOK, HEAD_DIM), BF16),
            jax.ShapeDtypeStruct((40, 2 * HALF), F32),
        ),
        in_specs=[smem, smem] + [hbm] * 4 + [vmem] * 3,
        out_specs=(hbm, vmem, hbm, vmem, vmem, vmem),
        scratch_shapes=list(SCRATCH.values()),
        compiler_params=pltpu.CompilerParams(
            collective_id=0, has_side_effects=True, vmem_limit_bytes=60 * 2**20
        ),
        cost_estimate=pl.CostEstimate(flops=12 * 10**9, bytes_accessed=10 * 2**20, transcendentals=0),
    )(
        lengths,
        labels,
        hidden_in[0, 0],
        queries[0, 0],
        key_states[0, 0],
        value_states[0, 0],
        out_weight.T,
        norm_gain,
        reward_head,
    )
    results = (layer_rows, grad_query, grad_keys, grad_values, grad_weight)
    shapes = tuple(jax.ShapeDtypeStruct(r.shape, r.dtype) for r in results)
    layer_rows, grad_query, grad_keys, grad_values, grad_weight, loss = pl.pallas_call(
        place,
        out_shape=shapes + (jax.ShapeDtypeStruct((1,), F32),),
        in_specs=[vmem] * 6,
        out_specs=(vmem,) * 5 + (smem,),
        cost_estimate=pl.CostEstimate(flops=0, bytes_accessed=4 * 2**20, transcendentals=0),
    )(*results, loss)
    return (
        layer_rows[None, None],
        loss,
        grad_query[None, None],
        grad_keys[None, None],
        grad_values[None, None],
        grad_weight.T,
    )


def solution(mesh):
    in_specs = (
        P("dp", "pair", "tensor", None),
        P("dp", "pair", None, "tensor"),
        P("dp", "pair", None, "tensor"),
        P("dp", "pair", None, "tensor"),
        P("tensor", ("pair", "dp")),
        P(),
        P(),
        P("dp", None),
        P("dp"),
    )
    out_specs = (
        P("dp", "pair", "tensor", None),
        P("dp"),
        P("dp", "pair", None, "tensor"),
        P("dp", "pair", None, "tensor"),
        P("dp", "pair", None, "tensor"),
        P("tensor", ("pair", "dp")),
    )
    return jax.shard_map(
        per_device, mesh=mesh, in_specs=in_specs, out_specs=out_specs, check_vma=False
    )
```

```python
from types import SimpleNamespace

import jax
import jax.numpy as jnp
from jax import lax
from jax.experimental import pallas as pl
from jax.experimental.pallas import tpu as pltpu
from jax.sharding import PartitionSpec as P

HEAD_DIM = 128
LOSS_SCALE = 1024.0
NORM_EPS = 1e-06
LOG2E = 1.4426950408889634

TOK = 384
WIDTH = 2560
HEADS = 8
NX, NY, NZ = 4, 4, 8
ROWS = TOK // NX
CHUNKS = 4
CW = WIDTH // CHUNKS
BLK = 80
HALF = 512
HR = ROWS // 2
HL = HALF // 2
LA = 384
LB = HALF - LA

MESH = pl.DeviceIdType.MESH
F32 = jnp.float32
BF16 = jnp.bfloat16

NT = (((1,), (1,)), ((), ()))
TN = (((0,), (0,)), ((), ()))
NN = (((1,), (0,)), ((), ()))


def mm(a, b, dims):
    return lax.dot_general(a, b, dims, preferred_element_type=F32)


def device(x, y, z, c):
    return (z // 4, x, y * 8 + lax.rem(z, 4) * 2 + c)


def rcopy(src, dst, send, recv, dev):
    return pltpu.make_async_remote_copy(
        src_ref=src, dst_ref=dst, send_sem=send, recv_sem=recv, device_id=dev, device_id_type=MESH
    )


DMA = pltpu.SemaphoreType.DMA
ARGS = (
    "lens",
    "labels",
    "hidden",
    "q",
    "k",
    "v",
    "wt",
    "gain",
    "head",
    "layer_o",
    "loss_o",
    "dq_o",
    "dk_o",
    "dv_o",
    "gw_o",
)
SCRATCH = dict(
    wh=pltpu.VMEM((2, 2, NY, 4, BLK, HALF), BF16),
    wf=pltpu.VMEM((2, 40, HALF), F32),
    qv=pltpu.VMEM((TOK, HEADS * HEAD_DIM), BF16),
    hv=pltpu.VMEM((ROWS, WIDTH), BF16),
    lv=pltpu.VMEM((ROWS, WIDTH), BF16),
    dqv=pltpu.VMEM((TOK, HEADS * HEAD_DIM), BF16),
    asm=pltpu.VMEM((BLK, HALF), F32),
    kall=pltpu.VMEM((2 * TOK, HEAD_DIM), BF16),
    vall=pltpu.VMEM((2 * TOK, HEAD_DIM), BF16),
    ktr=pltpu.VMEM((HEAD_DIM, 2 * TOK), BF16),
    vtr=pltpu.VMEM((HEAD_DIM, 2 * TOK), BF16),
    bias=pltpu.VMEM((2 * TOK, TOK), F32),
    peak=pltpu.VMEM((HEADS, 1, TOK), F32),
    mass=pltpu.VMEM((HEADS, 1, TOK), F32),
    part_out=pltpu.VMEM((HEADS, HEAD_DIM, TOK), F32),
    probs=pltpu.VMEM((HEADS, 2 * TOK, TOK), BF16),
    dscores=pltpu.VMEM((HEADS, 2 * TOK, TOK), BF16),
    lse=pltpu.VMEM((HEADS, 1, TOK), F32),
    att=pltpu.VMEM((2, TOK, HALF), BF16),
    acc=pltpu.VMEM((CHUNKS, NX, ROWS, CW), F32),
    xs=pltpu.VMEM((CHUNKS, NX, ROWS, CW), BF16),
    xin=pltpu.VMEM((2, CHUNKS, ROWS, CW), BF16),
    xrel=pltpu.VMEM((2, CHUNKS, HR, CW), BF16),
    xro=pltpu.VMEM((2, CHUNKS, HR, CW), BF16),
    gf=pltpu.VMEM((CHUNKS, NX, ROWS, CW), BF16),
    rw=pltpu.VMEM((2, NX, 8, 128), F32),
    own=pltpu.VMEM((CHUNKS, CW, HALF), F32),
    mo=pltpu.VMEM((CHUNKS, CW, HALF), BF16),
    mi=pltpu.VMEM((CHUNKS, CW, HALF), BF16),
    red=pltpu.VMEM((2, NY, 4, BLK, HALF), BF16),
    yin=pltpu.VMEM((2, 2, 4, BLK, LA), BF16),
    yrel=pltpu.VMEM((2, 2, 2, BLK, LA), BF16),
    yro=pltpu.VMEM((2, 2, 2, BLK, LA), BF16),
    zsend=pltpu.VMEM((2, 4, BLK, LA), BF16),
    zl=pltpu.VMEM((7, BLK, LA), BF16),
    z2l=pltpu.VMEM((2, 2, 2, 2, BLK, LB), BF16),
    z2third=pltpu.VMEM((2, 2, 2, BLK, LB), BF16),
    z2fourth=pltpu.VMEM((2, 2, 1, BLK, LB), BF16),
    z2out=pltpu.VMEM((2, 2, 2, BLK, LB), BF16),
    y2send=pltpu.VMEM((NY, BLK, LB), BF16),
    y2l=pltpu.VMEM((3, BLK, LB), BF16),
    factor=pltpu.VMEM((1, WIDTH), F32),
    gwc=pltpu.VMEM((BLK, HALF), F32),
    gwr=pltpu.VMEM((40, HALF), F32),
    gacc=pltpu.VMEM((2, TOK, HALF), F32),
    gatt=pltpu.VMEM((2, TOK, HALF), BF16),
    dk=pltpu.VMEM((2 * TOK, HEAD_DIM), F32),
    dv=pltpu.VMEM((2 * TOK, HEAD_DIM), F32),
    dkv_out=pltpu.VMEM((2, TOK, HEAD_DIM), BF16),
    dkv_in=pltpu.VMEM((2, TOK, HEAD_DIM), BF16),
    s_kv=DMA((4,)),
    r_kv=DMA((4,)),
    s_c=DMA((4,)),
    r_c=DMA((4,)),
    s_z=DMA((8,)),
    r_z=DMA((8,)),
    s_w=DMA((8,)),
    r_w=DMA((8,)),
    s_y=DMA((4, 8)),
    r_y=DMA((4, 8)),
    s_x=DMA((3, 2, CHUNKS)),
    r_x=DMA((3, 2, CHUNKS)),
    s_g=DMA((2, 2, CHUNKS)),
    r_g=DMA((2, 2, CHUNKS)),
    s_rw=DMA((4,)),
    r_rw=DMA((4,)),
    s_m=DMA((CHUNKS,)),
    r_m=DMA((CHUNKS,)),
    t_z=DMA((7,)),
    u_z=DMA((7,)),
    t_y=DMA((3, 2, 2)),
    u_y=DMA((3, 2, 2)),
    t_z2=DMA((4, 2, 2)),
    u_z2=DMA((4, 2, 2)),
    loc=DMA((8,)),
    out_l=DMA((CHUNKS,)),
    out_q=DMA((HEADS,)),
    t_y2=DMA((3,)),
    u_y2=DMA((3,)),
)


def kernel(*refs):
    names = SimpleNamespace(**dict(zip(ARGS + tuple(SCRATCH), refs)))
    run(names)


def run(n):
    lens = n.lens
    labels = n.labels
    hidden = n.hidden
    q = n.q
    k = n.k
    v = n.v
    wt = n.wt
    gain = n.gain
    head = n.head
    layer_o = n.layer_o
    loss_o = n.loss_o
    dq_o = n.dq_o
    dk_o = n.dk_o
    dv_o = n.dv_o
    gw_o = n.gw_o
    wh = n.wh
    wf = n.wf
    qv = n.qv
    hv = n.hv
    lv = n.lv
    dqv = n.dqv
    asm = n.asm
    kall = n.kall
    vall = n.vall
    ktr = n.ktr
    vtr = n.vtr
    bias = n.bias
    peak = n.peak
    mass = n.mass
    part_out = n.part_out
    probs = n.probs
    dscores = n.dscores
    lse = n.lse
    att = n.att
    acc = n.acc
    xs = n.xs
    xin = n.xin
    xrel = n.xrel
    xro = n.xro
    gf = n.gf
    rw = n.rw
    own = n.own
    mo = n.mo
    mi = n.mi
    red = n.red
    yin = n.yin
    yrel = n.yrel
    yro = n.yro
    zsend = n.zsend
    zl = n.zl
    z2l = n.z2l
    z2third = n.z2third
    z2fourth = n.z2fourth
    z2out = n.z2out
    y2send = n.y2send
    y2l = n.y2l
    factor = n.factor
    gwc = n.gwc
    gwr = n.gwr
    gacc = n.gacc
    gatt = n.gatt
    dk = n.dk
    dv = n.dv
    dkv_out = n.dkv_out
    dkv_in = n.dkv_in
    s_kv = n.s_kv
    r_kv = n.r_kv
    s_c = n.s_c
    r_c = n.r_c
    s_z = n.s_z
    r_z = n.r_z
    s_w = n.s_w
    r_w = n.r_w
    s_y = n.s_y
    r_y = n.r_y
    s_x = n.s_x
    r_x = n.r_x
    s_g = n.s_g
    r_g = n.r_g
    s_rw = n.s_rw
    r_rw = n.r_rw
    s_m = n.s_m
    r_m = n.r_m
    t_z = n.t_z
    u_z = n.u_z
    t_y = n.t_y
    u_y = n.u_y
    t_z2 = n.t_z2
    u_z2 = n.u_z2
    loc = n.loc
    out_l = n.out_l
    out_q = n.out_q
    t_y2 = n.t_y2
    u_y2 = n.u_y2

    pair = lax.axis_index("pair")
    x = lax.axis_index("tensor")
    dp = lax.axis_index("dp")
    y = dp // 8
    zlo = lax.rem(dp // 2, 4)
    z = pair * 4 + zlo
    c = lax.rem(dp, 2)
    mate = 1 - c

    def xdev(d):
        return device(lax.rem(x + d, NX), y, z, c)

    def ydev(d):
        return device(x, lax.rem(y + d, NY), z, c)

    def zdev(d):
        return device(x, y, lax.rem(z + d, NZ), c)

    core = device(x, y, z, mate)
    far = zdev(4)

    local = [
        pltpu.make_async_copy(k, kall.at[pl.ds(0, TOK)], loc.at[0]),
        pltpu.make_async_copy(v, vall.at[pl.ds(0, TOK)], loc.at[1]),
        pltpu.make_async_copy(q, qv, loc.at[2]),
    ]
    load_hidden = pltpu.make_async_copy(hidden, hv, loc.at[3])
    for cp in local + [load_hidden]:
        cp.start()

    barrier = pltpu.get_barrier_semaphore()
    peers = [core]
    peers += [xdev(d) for d in (1, 2, 3)]
    peers += [ydev(d) for d in (1, 2, 3)]
    peers += [zdev(d) for d in range(1, NZ)]
    for peer in peers:
        pl.semaphore_signal(barrier, inc=1, device_id=peer, device_id_type=MESH)

    len_own = jnp.where(pair == 0, lens[0, 0], lens[0, 1])
    len_par = jnp.where(pair == 0, lens[0, 1], lens[0, 0])
    key_id = lax.broadcasted_iota(jnp.int32, (TOK, TOK), 0)
    tok_id = lax.broadcasted_iota(jnp.int32, (TOK, TOK), 1)
    bias[0:TOK, :] = jnp.where((key_id <= tok_id) & (key_id < len_own), 0.0, -1e30)
    bias[TOK:, :] = jnp.where(key_id < len_par, 0.0, -1e30)

    for half in range(2):
        wf[half] = wt[:, pl.ds(half * HALF, HALF)].astype(F32)

    factor[...] = (gain[...] * head[...]).reshape(1, WIDTH)

    pl.semaphore_wait(barrier, len(peers))

    kv_copies = [
        rcopy(k, kall.at[pl.ds(TOK, TOK)], s_kv.at[0], r_kv.at[0], far),
        rcopy(v, vall.at[pl.ds(TOK, TOK)], s_kv.at[1], r_kv.at[1], far),
    ]
    mine = pl.ds(pl.multiple_of(c * 40, 8), 40)
    wcore = rcopy(wf.at[mate], asm.at[mine], s_c.at[0], r_c.at[0], core)
    wcore.start()

    asm[mine, :] = wf[c]
    wcore.wait()
    wh[c, pair, y, zlo] = asm[...].astype(BF16)

    steps = (0, 7, 1, 6, 2, 5, 3, 4)

    def hop(e):
        there = lax.rem(pair + e // 4, 2) * 4 + lax.rem(zlo + e, 4)
        return there, lax.rem(there - z + NZ, NZ)

    def block(row, e):
        there = lax.rem(z + steps[e], NZ)
        return wh.at[c, there // 4, row, lax.rem(there, 4)]

    def zcopy(e):
        part = block(y, 0 if e <= 2 else e - 2)
        return rcopy(part, part, s_z.at[e], r_z.at[e], zdev(1 if e % 2 else 7))

    def ycopy(s, e):
        part = block(y, e)
        return rcopy(part, part, s_y.at[s, e], r_y.at[s, e], ydev(1 + 2 * s))

    def ypass(s, e):
        part = block(lax.rem(y + 3 - 2 * s, NY), e).at[:, pl.ds(s * HL, HL)]
        return rcopy(part, part, s_y.at[2 + s, e], r_y.at[2 + s, e], ydev(1 + 2 * s))

    def swap(e):
        there = lax.rem(z + steps[e], NZ)
        part = wh.at[c, there // 4, :, lax.rem(there, 4)]
        return rcopy(part, part, s_w.at[e], r_w.at[e], core)

    def yforward(e):
        for s in range(2):
            ycopy(s, e).wait_recv()
        for s in range(2):
            ypass(s, e).start()

    def hand(e):
        for s in range(2):
            ypass(s, e).wait_recv()
        swap(e).start()

    def serve(e):
        zcopy(e).wait_recv()
        if e + 2 < 8:
            zcopy(e + 2).start()
        for s in range(2):
            ycopy(s, e).start()
        yforward(e - 1)
        if e == 2:
            for cp in kv_copies:
                cp.start()
        if e >= 3:
            hand(e - 3)

    for e in (1, 2):
        zcopy(e).start()
    for s in range(2):
        ycopy(s, 0).start()

    scale2 = HEAD_DIM ** (-0.5) * LOG2E
    for cp in local:
        cp.wait()
    ktr[:, 0:TOK] = jnp.transpose(kall[0:TOK, :].astype(F32)).astype(BF16)
    vtr[:, 0:TOK] = jnp.transpose(vall[0:TOK, :].astype(F32)).astype(BF16)

    def softmax_part(h, rows):
        cols = pl.ds(pl.multiple_of(h * HEAD_DIM, HEAD_DIM), HEAD_DIM)
        s = mm(kall[rows, :], qv[:, cols], NT) * scale2 + bias[rows, :]
        top = jnp.max(s, axis=0, keepdims=True)
        e = jnp.exp2(s - top)
        total = jnp.sum(e, axis=0, keepdims=True)
        return top, total, mm(vtr[:, rows], e.astype(BF16), NN)

    def forward_own(h, carry):
        peak[h], mass[h], part_out[h] = softmax_part(h, pl.ds(0, TOK))
        return carry

    def forward_far(h, carry):
        top1, total1, out1 = peak[h], mass[h], part_out[h]
        top2, total2, out2 = softmax_part(h, pl.ds(TOK, TOK))
        top = jnp.maximum(top1, top2)
        fac1, fac2 = jnp.exp2(top1 - top), jnp.exp2(top2 - top)
        total = total1 * fac1 + total2 * fac2
        out = out1 * (fac1 / total) + out2 * (fac2 / total)
        lane = pl.ds(pl.multiple_of(lax.rem(h, 4) * HEAD_DIM, HEAD_DIM), HEAD_DIM)
        att[h // 4, :, lane] = jnp.transpose(out).astype(BF16)
        lse[h] = top + jnp.log2(total)
        return carry

    for e in range(1, 7):
        lax.fori_loop(e - 1, e, forward_own, 0)
        serve(e)
    lax.fori_loop(6, HEADS, forward_own, 0)
    serve(7)
    for cp in kv_copies:
        cp.wait()
    ktr[:, TOK:] = jnp.transpose(kall[TOK:, :].astype(F32)).astype(BF16)
    vtr[:, TOK:] = jnp.transpose(vall[TOK:, :].astype(F32)).astype(BF16)
    lax.fori_loop(0, 2, forward_far, 0)
    yforward(7)
    hand(5)
    lax.fori_loop(2, HEADS, forward_far, 0)
    hand(6)

    def wrows(half, j):
        return wh[half, j // 2, pl.ds(lax.rem(j, 2) * 2, 2)].reshape(CW, HALF)

    def project_own(i, carry):
        j = lax.rem(i + 2 * pair, CHUNKS)
        acc[j] = mm(att[c], wrows(c, j), NT).reshape(NX, ROWS, CW)
        return carry

    def xcopy(kind, t, j):
        near = 1 + 2 * t
        if kind == 0:
            src, dst = xs.at[j, lax.rem(x + 2, NX), pl.ds(HR * t, HR)], xrel.at[t, j]
        elif kind == 1:
            rows = pl.ds(HR * (1 - t), HR)
            src, dst = xs.at[j, lax.rem(x + near, NX), rows], xin.at[t, j, rows]
        else:
            src, dst = xro.at[t, j], xin.at[t, j, pl.ds(HR * t, HR)]
        return rcopy(src, dst, s_x.at[kind, t, j], r_x.at[kind, t, j], xdev(near))

    def xstart(i):
        j = lax.rem(i + 2 * pair, CHUNKS)
        for kind in range(2):
            for t in range(2):
                xcopy(kind, t, j).start()

    def xsent(i):
        j = lax.rem(i + 2 * pair, CHUNKS)
        for kind in range(2):
            for t in range(2):
                xcopy(kind, t, j).wait_send()

    def project_rest(i, carry):
        j = lax.rem(i + 2 * pair, CHUNKS)
        p = acc[j] + mm(att[mate], wrows(mate, j), NT).reshape(NX, ROWS, CW)
        acc[j] = p
        xs[j] = p.astype(BF16)
        return carry

    def xforward(i, carry):
        j = lax.rem(i + 2 * pair, CHUNKS)
        for t in range(2):
            xcopy(0, t, j).wait_recv()
            mine_too = acc[j, lax.rem(x + 1 + 2 * t, NX), pl.ds(HR * t, HR)]
            xro[t, j] = (mine_too + xrel[t, j].astype(F32)).astype(BF16)
            xcopy(2, t, j).start()
        return carry

    def probability(h, carry):
        cols = pl.ds(pl.multiple_of(h * HEAD_DIM, HEAD_DIM), HEAD_DIM)
        s = mm(kall[...], qv[:, cols], NT) * scale2 + bias[...]
        probs[h] = jnp.exp2(s - lse[h]).astype(BF16)
        return carry

    lax.fori_loop(0, 2, project_own, 0)
    for e in range(7):
        swap(e).wait()
    project_rest(0, 0)
    xstart(0)
    project_rest(1, 0)
    hand(7)
    lax.fori_loop(2, CHUNKS, project_own, 0)
    swap(7).wait()
    lax.fori_loop(2, CHUNKS, project_rest, 0)

    def xstep(i, carry):
        xstart(i)
        xforward(i - 1, 0)
        xsent(i - 1)
        lax.fori_loop(2 * i - 2, 2 * i, probability, 0)
        return carry

    lax.fori_loop(1, CHUNKS, xstep, 0)
    xsent(CHUNKS - 1)
    xforward(CHUNKS - 1, 0)
    lax.fori_loop(6, HEADS, probability, 0)
    for e in range(8):
        if e > 0:
            zcopy(e).wait_send()
        for s in range(2):
            ycopy(s, e).wait_send()
            ypass(s, e).wait_send()
    load_hidden.wait()

    def layer_copy(j):
        cols = pl.ds(pl.multiple_of(j * CW, 128), CW)
        return pltpu.make_async_copy(lv.at[:, cols], layer_o.at[:, cols], out_l.at[j])

    def layer(i, carry):
        square, along = carry
        j = lax.rem(i + 2 * pair, CHUNKS)
        for t in range(2):
            xcopy(1, t, j).wait_recv()
            xcopy(2, t, j).wait()
        cols = pl.ds(pl.multiple_of(j * CW, 128), CW)
        total = hv[:, cols].astype(F32) + acc[j, x]
        for t in range(2):
            total += xin[t, j].astype(F32)
        rounded = total.astype(BF16)
        lv[:, cols] = rounded
        layer_copy(j).start()
        value = rounded.astype(F32)
        square += jnp.sum(value * value, axis=1, keepdims=True)
        along += jnp.sum(value * factor[:, cols], axis=1, keepdims=True)
        return square, along

    zero = jnp.zeros((ROWS, 1), F32)
    square, along = lax.fori_loop(0, CHUNKS, layer, (zero, zero))
    inv = lax.rsqrt(square * (1.0 / WIDTH) + NORM_EPS)
    position = x * ROWS + lax.broadcasted_iota(jnp.int32, (ROWS, 1), 0)
    valid = jnp.where(position < len_own, 1.0, 0.0)
    root = jnp.sqrt(jnp.full((ROWS, 1), len_own, jnp.int32).astype(F32))
    weight = valid / root
    partial = jnp.sum(inv * along * weight, axis=0, keepdims=True)
    rw[pair, x] = jnp.broadcast_to(partial, (8, 128))
    own_rw = rw.at[pair, x]
    rw_far = rcopy(own_rw, own_rw, s_rw.at[0], r_rw.at[0], far)
    rw_far.start()
    both_rw = rw.at[:, x]
    rw_copies = [rcopy(both_rw, both_rw, s_rw.at[d], r_rw.at[d], xdev(d)) for d in (1, 2, 3)]

    gscale = inv * weight
    gcorr = inv * inv * inv * along * weight * (1.0 / WIDTH)

    def gcopy(kind, t, j):
        if kind == 0:
            part = gf.at[j, x]
        else:
            part = gf.at[j, lax.rem(x + 3 - 2 * t, NX), pl.ds(HR * t, HR)]
        return rcopy(part, part, s_g.at[kind, t, j], r_g.at[kind, t, j], xdev(1 + 2 * t))

    def rows_grad(i, carry):
        j = i
        cols = pl.ds(pl.multiple_of(j * CW, 128), CW)
        value = lv[:, cols].astype(F32)
        gf[j, x] = (gscale * factor[:, cols] - value * gcorr).astype(BF16)
        for t in range(2):
            @pl.when(i < 1)
            def _():
                gcopy(0, t, j).start()
        return carry

    lax.fori_loop(0, CHUNKS, rows_grad, 0)

    def gforward(i):
        j = i
        for t in range(2):
            gcopy(0, t, j).wait_send()
        if i + 1 < CHUNKS:
            for t in range(2):
                gcopy(0, t, lax.rem(j + 1, CHUNKS)).start()
        for t in range(2):
            gcopy(0, t, j).wait_recv()
        for t in range(2):
            gcopy(1, t, j).start()

    rw_far.wait()
    for cp in rw_copies:
        cp.start()
    gforward(0)
    gforward(1)
    for cp in rw_copies:
        cp.wait()
    reward0 = rw[0, 0] + rw[0, 1] + rw[0, 2] + rw[0, 3]
    reward1 = rw[1, 0] + rw[1, 1] + rw[1, 2] + rw[1, 3]
    sign = 2.0 * jnp.full((8, 128), labels[0], jnp.int32).astype(F32) - 1.0
    margin = sign * (reward0 - reward1)
    loss_o[...] = jnp.maximum(-margin, 0.0) + jnp.log1p(jnp.exp(-jnp.abs(margin)))
    first = -sign * jax.nn.sigmoid(-margin) * LOSS_SCALE
    side = jnp.where(pair == 0, 1.0, -1.0)
    slope = (first * side)[0:1, 0:1]

    def mcopy(j):
        return rcopy(mo.at[j], mi.at[j], s_m.at[j], r_m.at[j], core)

    gacc[...] = jnp.zeros_like(gacc)

    def products(i):
        j = i
        for t in range(2):
            gcopy(1, t, j).wait()
        g = gf[j].reshape(TOK, CW)
        mo[j] = (mm(g, att[mate], TN) * slope).astype(BF16)
        mcopy(j).start()
        own[j] = mm(g, att[c], TN) * slope
        for half in range(2):
            gacc[half] += mm(g, wrows(half, j), NN)

    def ycopy2(kind, s, zh):
        near = 1 + 2 * s
        if kind == 0:
            src = red.at[zh, lax.rem(y + 2, NY), pl.ds(2 * s, 2), :, pl.ds(0, LA)]
            dst = yrel.at[s, zh]
        elif kind == 1:
            blocks = pl.ds(2 - 2 * s, 2)
            src = red.at[zh, lax.rem(y + near, NY), blocks, :, pl.ds(0, LA)]
            dst = yin.at[s, zh, blocks]
        else:
            src, dst = yro.at[s, zh], yin.at[s, zh, pl.ds(2 * s, 2)]
        return rcopy(src, dst, t_y.at[kind, s, zh], u_y.at[kind, s, zh], ydev(near))

    def zblock(d, yp):
        to = lax.rem(z + d, NZ)
        return to // 4, pl.ds(2 * yp, 2), lax.rem(to, 4), slice(None), pl.ds(LA, LB)

    def zcopy3(kind, s, yp):
        near, over = (1, NZ - 1)[s], (2, NZ - 2)[s]
        sems = t_z2.at[kind, s, yp], u_z2.at[kind, s, yp]
        if kind == 0:
            return rcopy(red.at[zblock(near, yp)], z2l.at[s, 0, yp], *sems, zdev(near))
        if kind == 1:
            return rcopy(red.at[zblock((3, 5)[s], yp)], z2third.at[s, yp], *sems, zdev(near))
        if kind == 2:
            to = lax.rem(z + 4, NZ)
            src = red.at[to // 4, pl.ds(2 * yp + s, 1), lax.rem(to, 4), :, pl.ds(LA, LB)]
            return rcopy(src, z2fourth.at[s, yp], *sems, zdev(over))
        return rcopy(z2out.at[s, yp], z2l.at[s, 1, yp], *sems, zdev(over))

    def zrelay(i):
        zh, yp = i // 2, i % 2
        for s in range(2):
            over = (2, NZ - 2)[s]

            @pl.when(lax.rem(z + over, NZ) // 4 == zh)
            def _():
                zcopy3(1, s, yp).wait_recv()
                zcopy3(2, s, yp).wait_recv()
                both = red[zblock(over, yp)].astype(F32) + z2third[s, yp].astype(F32)
                z2out[s, yp, 1 - s] = both[1 - s].astype(BF16)
                z2out[s, yp, s] = (both[s] + z2fourth[s, yp, 0].astype(F32)).astype(BF16)
                zcopy3(3, s, yp).start()

    def merge(i):
        j = i
        zh, yp = j // 2, j % 2
        mcopy(j).wait()
        both = own[j] + mi[j].astype(F32)
        red[zh, pl.ds(yp * 2, 2)] = both.astype(BF16).reshape(2, 4, BLK, HALF)

        @pl.when(lax.rem(y + 2, NY) // 2 == yp)
        def _():
            for s in range(2):
                ycopy2(0, s, zh).start()

        for s in range(2):
            @pl.when(lax.rem(y + 1 + 2 * s, NY) // 2 == yp)
            def _():
                ycopy2(1, s, zh).start()

        for kind, spans in ((2, (4, 4)), (1, (3, 5)), (0, (1, 7))):
            for s in range(2):
                @pl.when(lax.rem(z + spans[s], NZ) // 4 == zh)
                def _():
                    zcopy3(kind, s, yp).start()

    def yrelay(zh):
        for s in range(2):
            ycopy2(0, s, zh).wait_recv()
            mine_too = red[zh, lax.rem(y + 1 + 2 * s, NY), pl.ds(2 * s, 2), :, pl.ds(0, LA)].astype(F32)
            yro[s, zh] = (mine_too + yrel[s, zh].astype(F32)).astype(BF16)
            ycopy2(2, s, zh).start()

    products(0)
    gforward(2)
    products(1)
    merge(0)
    gforward(3)
    products(2)
    merge(1)
    zrelay(0)
    products(3)
    merge(2)
    zrelay(1)
    merge(3)

    gatt[...] = gacc[...].astype(BF16)
    dk[...] = jnp.zeros_like(dk)
    dv[...] = jnp.zeros_like(dv)
    slope_scaled = slope * HEAD_DIM ** (-0.5)

    def dq_copy(h):
        cols = pl.ds(pl.multiple_of(h * HEAD_DIM, HEAD_DIM), HEAD_DIM)
        return pltpu.make_async_copy(dqv.at[:, cols], dq_o.at[:, cols], out_q.at[h])

    def backward(h, carry):
        cols = pl.ds(pl.multiple_of(h * HEAD_DIM, HEAD_DIM), HEAD_DIM)
        lane = pl.ds(pl.multiple_of(lax.rem(h, 4) * HEAD_DIM, HEAD_DIM), HEAD_DIM)
        gh = gatt[h // 4, :, lane]
        p = probs[h].astype(F32)
        dprob = mm(vall[...], gh, NT)
        delta = jnp.sum(p * dprob, axis=0, keepdims=True)
        dscores[h] = (p * (dprob - delta)).astype(BF16)
        dv[...] += mm(probs[h], gh, NN)
        dk[TOK:, :] += mm(dscores[h, TOK:, :], qv[:, cols], NN)
        return carry

    def backward_rest(h, carry):
        cols = pl.ds(pl.multiple_of(h * HEAD_DIM, HEAD_DIM), HEAD_DIM)
        dk[0:TOK, :] += mm(dscores[h, 0:TOK, :], qv[:, cols], NN)
        dqv[:, cols] = (jnp.transpose(mm(ktr[...], dscores[h], NN)) * slope_scaled).astype(BF16)
        dq_copy(h).start()
        return carry

    def zcopy2(d):
        to = lax.rem(z + d, NZ)
        src = zsend.at[to // 4, lax.rem(to, 4)]
        return rcopy(src, zl.at[d - 1], t_z.at[d - 1], u_z.at[d - 1], zdev(d))

    def ysum(zh):
        total = red[zh, y, :, :, pl.ds(0, LA)].astype(F32)
        for s in range(2):
            ycopy2(1, s, zh).wait_recv()
            ycopy2(2, s, zh).wait_recv()
            total += yin[s, zh].astype(F32)
        zsend[zh] = total.astype(BF16)

        @pl.when(pair != zh)
        def _():
            zcopy2(4).start()

        for e in (1, 2, 3):
            there = zh * 4 + lax.rem(zlo + e, 4)
            zcopy2(lax.rem(there - z + NZ, NZ)).start()

    lax.fori_loop(0, 3, backward, 0)
    zrelay(2)
    yrelay(0)
    lax.fori_loop(3, 5, backward, 0)
    zrelay(3)
    lax.fori_loop(5, HEADS, backward, 0)

    dkv_out[0] = (dk[TOK:, :] * slope_scaled).astype(BF16)
    dkv_out[1] = (dv[TOK:, :] * slope).astype(BF16)
    back = [rcopy(dkv_out.at[i], dkv_in.at[i], s_kv.at[2 + i], r_kv.at[2 + i], far) for i in range(2)]
    for cp in back:
        cp.start()

    yrelay(1)
    ysum(0)
    lax.fori_loop(0, HEADS, backward_rest, 0)
    ysum(1)
    total = red[pair, :, zlo, :, pl.ds(LA, LB)].astype(F32).reshape(2, 2, BLK, LB)
    for s in range(2):
        for kind in range(4):
            for yp in range(2):
                zcopy3(kind, s, yp).wait_send()
                if kind % 3 == 0:
                    zcopy3(kind, s, yp).wait_recv()
        for kind in range(2):
            total += z2l[s, kind].astype(F32)
    y2send[...] = total.astype(BF16).reshape(NY, BLK, LB)
    yb2 = []
    for d in (2, 1, 3):
        src = y2send.at[lax.rem(y + d, NY)]
        yb2.append(rcopy(src, y2l.at[d - 1], t_y2.at[d - 1], u_y2.at[d - 1], ydev(d)))
        yb2[-1].start()
    for d in range(1, 8):
        zcopy2(d).wait()
    for kind in range(3):
        for s in range(2):
            for zh in range(2):
                ycopy2(kind, s, zh).wait_send()
    total = zsend[pair, zlo].astype(F32)
    for d in range(7):
        total += zl[d].astype(F32)
    gwc[:, 0:LA] = total
    for cp in yb2:
        cp.wait()
    total = y2send[y].astype(F32)
    for d in range(3):
        total += y2l[d].astype(F32)
    gwc[:, LA:] = total
    mate_rows = gwc.at[pl.ds(pl.multiple_of(mate * 40, 8), 40)]
    gswap = rcopy(mate_rows, gwr, s_c.at[3], r_c.at[3], core)
    gswap.start()
    gw_o[:, pl.ds(pl.multiple_of(c * HALF, HALF), HALF)] = gwc[mine, :]
    gswap.wait()
    gw_o[:, pl.ds(pl.multiple_of(mate * HALF, HALF), HALF)] = gwr[...]

    for j in range(CHUNKS):
        layer_copy(j).wait()
    for h in range(HEADS):
        dq_copy(h).wait()
    for cp in back:
        cp.wait()
    dk_o[...] = (dk[0:TOK, :] * slope_scaled + dkv_in[0].astype(F32)).astype(BF16)
    dv_o[...] = (dv[0:TOK, :] * slope + dkv_in[1].astype(F32)).astype(BF16)


def place(*refs):
    for source, result in zip(refs[:5], refs[6:]):
        result[...] = source[...]
    refs[11][0] = jnp.max(refs[5][...])


def per_device(hidden_in, queries, key_states, value_states, out_weight, norm_gain, reward_head, lengths, labels):
    smem = pl.BlockSpec(memory_space=pltpu.SMEM)
    vmem = pl.BlockSpec(memory_space=pltpu.VMEM)
    hbm = pl.BlockSpec(memory_space=pl.ANY)
    layer_rows, loss, grad_query, grad_keys, grad_values, grad_weight = pl.pallas_call(
        kernel,
        out_shape=(
            jax.ShapeDtypeStruct((ROWS, WIDTH), BF16),
            jax.ShapeDtypeStruct((8, 128), F32),
            jax.ShapeDtypeStruct((TOK, HEADS * HEAD_DIM), BF16),
            jax.ShapeDtypeStruct((TOK, HEAD_DIM), BF16),
            jax.ShapeDtypeStruct((TOK, HEAD_DIM), BF16),
            jax.ShapeDtypeStruct((40, 2 * HALF), F32),
        ),
        in_specs=[smem, smem] + [hbm] * 4 + [vmem] * 3,
        out_specs=(hbm, vmem, hbm, vmem, vmem, vmem),
        scratch_shapes=list(SCRATCH.values()),
        compiler_params=pltpu.CompilerParams(
            collective_id=0, has_side_effects=True, vmem_limit_bytes=60 * 2**20
        ),
        cost_estimate=pl.CostEstimate(flops=12 * 10**9, bytes_accessed=10 * 2**20, transcendentals=0),
    )(
        lengths,
        labels,
        hidden_in[0, 0],
        queries[0, 0],
        key_states[0, 0],
        value_states[0, 0],
        out_weight.T,
        norm_gain,
        reward_head,
    )
    results = (layer_rows, grad_query, grad_keys, grad_values, grad_weight)
    shapes = tuple(jax.ShapeDtypeStruct(r.shape, r.dtype) for r in results)
    layer_rows, grad_query, grad_keys, grad_values, grad_weight, loss = pl.pallas_call(
        place,
        out_shape=shapes + (jax.ShapeDtypeStruct((1,), F32),),
        in_specs=[vmem] * 6,
        out_specs=(vmem,) * 5 + (smem,),
        cost_estimate=pl.CostEstimate(flops=0, bytes_accessed=4 * 2**20, transcendentals=0),
    )(*results, loss)
    return (
        layer_rows[None, None],
        loss,
        grad_query[None, None],
        grad_keys[None, None],
        grad_values[None, None],
        grad_weight.T,
    )


def solution(mesh):
    in_specs = (
        P("dp", "pair", "tensor", None),
        P("dp", "pair", None, "tensor"),
        P("dp", "pair", None, "tensor"),
        P("dp", "pair", None, "tensor"),
        P("tensor", ("pair", "dp")),
        P(),
        P(),
        P("dp", None),
        P("dp"),
    )
    out_specs = (
        P("dp", "pair", "tensor", None),
        P("dp"),
        P("dp", "pair", None, "tensor"),
        P("dp", "pair", None, "tensor"),
        P("dp", "pair", None, "tensor"),
        P("tensor", ("pair", "dp")),
    )
    return jax.shard_map(
        per_device, mesh=mesh, in_specs=in_specs, out_specs=out_specs, check_vma=False
    )
```
